256 devices in a mesh: ctx: 8 (over x, core), tp: 32 (over z, y).
Axes of the slice: x: 4, y: 4, z: 8, core: 2. Of those that a mesh axis runs over, the one named last changes fastest.
Arguments:
- tokens: bfloat16 [2048, 8192], P('ctx', 'tp'), may hold values from -6 to 6
- in_weight: bfloat16 [3, 8192, 8192], P(None, 'ctx', 'tp'), may hold values from -0.0625 to 0.0625
- filter_spectrum: float32 [2, 16, 256, 8192], P(None, 'ctx', None, 'tp'), may hold values from -6 to 6
- skip_gain: float32 [8192], P('tp'), may hold values from -4 to 4
- out_weight: bfloat16 [8192, 8192], P(None, 'tp'), may hold values from -0.0625 to 0.0625
Outputs:
- mixed: bfloat16 [2048, 8192], P('ctx', 'tp')
The draws below stay inside these ranges and needn't reach their ends.
All inputs are finite; a program needn't handle non-finite values.
Results may differ from the reference program's by a relative error of at most 0.007.
Values may be sent and summed in bfloat16 or wider, within the bound.
No kernel may reach another device: no remote copies, remote signals or barrier semaphores. Data moves between devices by JAX's collectives and lax.ppermute only.
A program may use at most 128 MiB of HBM per device.

```python
import jax
import jax.numpy as jnp

D = 8192
TOK_DEV = 256
SEQ = 2048
BLOCKS = 16


def block_levels(rng, dims, split, low, high):
    loudness = 1.0
    for dim, parts in split:
        draws = jax.random.uniform(jax.random.fold_in(jax.random.fold_in(rng, 6), dim), (parts,), jnp.float32, low / len(split), high / len(split))
        loudness = loudness * jnp.repeat(jnp.exp(draws), dims[dim] // parts).reshape((-1,) + (1,) * (len(dims) - 1 - dim))
    return loudness


def bell_draw(own_key, shape, deviation, limit, split=(), held_as=jnp.bfloat16):
    values = jax.random.normal(own_key, shape, jnp.float32) * deviation
    if len(split) > 0:
        values = block_levels(own_key, shape, split, -0.22, 0.18) * values
    return jnp.clip(values, min=-limit, max=limit).astype(held_as)


def setup_inputs(seed: int = 0) -> dict:
    key_of = jax.random.split(jax.random.key(seed), 6)
    tokens = bell_draw(key_of[0], (SEQ, D), 1.0, 6.0, ((0, 8), (1, 32)))
    in_weight = bell_draw(key_of[1], (3, D, D), D ** -0.5, 0.0625, ((1, 8), (2, 32)))
    filter_spectrum = bell_draw(key_of[2], (2, BLOCKS, TOK_DEV, D), 1.0, 6.0, ((1, 8), (3, 32)), jnp.float32)
    skip_gain = bell_draw(key_of[3], (D,), 1.0, 4.0, ((0, 32),), jnp.float32)
    out_weight = bell_draw(key_of[4], (D, D), D ** -0.5, 0.0625, ((1, 32),))
    return dict(tokens=tokens, in_weight=in_weight, filter_spectrum=filter_spectrum, skip_gain=skip_gain, out_weight=out_weight)


def reference(tokens, in_weight, filter_spectrum, skip_gain, out_weight):
    projected = [jnp.dot(tokens, in_weight[index], preferred_element_type=jnp.float32).astype(jnp.bfloat16) for index in range(3)]
    outer_gate = projected[0].astype(jnp.float32)
    inner_gate = projected[1].astype(jnp.float32)
    value_part = projected[2].astype(jnp.float32)
    driven = inner_gate * value_part
    padded = jnp.concatenate([driven, jnp.zeros_like(driven)], axis=0)
    signal_freq = jnp.fft.fft(padded, axis=0)
    total = 2 * SEQ
    filter_real = jnp.transpose(filter_spectrum[0], (1, 0, 2)).reshape(total, D)
    filter_imag = jnp.transpose(filter_spectrum[1], (1, 0, 2)).reshape(total, D)
    product = signal_freq * (filter_real + 1j * filter_imag)
    convolved = jnp.real(jnp.fft.ifft(product, axis=0))[:SEQ].astype(jnp.float32)
    gated = (outer_gate * (convolved + skip_gain * driven)).astype(jnp.bfloat16)
    return jnp.dot(gated, out_weight, preferred_element_type=jnp.float32).astype(jnp.bfloat16)
```

```python
import functools
import math

import jax
import jax.numpy as jnp
import numpy as np
from jax import lax
from jax.experimental import pallas as pl
from jax.experimental.pallas import tpu as pltpu
from jax.sharding import Mesh, PartitionSpec as P

NX, NC, NZ, NY = 4, 2, 8, 4
SIZES = dict(x=NX, core=NC, z=NZ, y=NY)
EVERY = ("x", "core", "z", "y")
CTX = ("x", "core")
HALF_CLASSES = 9


def place(x, core, z, y):
    return ((x * NC + core) * NZ + z) * NY + y


MOVE = [
    (place(p, core, 2 * x + f, y), place(x, core, 2 * p + f, y))
    for p in range(4)
    for core in range(2)
    for x in range(4)
    for f in range(2)
    for y in range(4)
]


def shift(values, axis, step):
    n = SIZES[axis]
    return lax.ppermute(values, axis, [(i, (i + step) % n) for i in range(n)])


def ring(values, axis):
    n = SIZES[axis]
    half = values.shape[0] // 2
    out = {0: values}
    up = down = values
    for k in range(1, n // 2):
        up, down = shift(up, axis, 1), shift(down, axis, -1)
        out[n - k], out[k] = up, down
    out[n // 2] = jnp.concatenate([shift(up[:half], axis, 1), shift(down[half:], axis, -1)], 0)
    return [out[k] for k in range(n)]


@functools.lru_cache(None)
def tables():
    r = np.arange(256)
    big = 2 * np.pi * (np.outer(r, r) % 256) / 256
    c, s = np.cos(big), np.sin(big)
    forward = np.block([[c, -s], [s, c]]).astype(np.float32)
    back = np.block([[c, s], [-s, c]]).astype(np.float32)
    j = np.arange(HALF_CLASSES)
    turn = 2 * np.pi * np.outer(j, r) / 4096
    twist = np.concatenate([np.cos(turn), np.sin(turn)], 1).astype(np.float32)
    return forward, back, twist[:, None, :]


def small(j, q):
    turn = 2 * math.pi * ((j * q) % 16) / 16
    return round(math.cos(turn), 12), round(math.sin(turn), 12)


def weighted(terms):
    total = None
    for scale, value in terms:
        if scale == 0.0:
            continue
        part = value if scale == 1.0 else -value if scale == -1.0 else scale * value
        total = part if total is None else total + part
    return total


def filter_kernel(
    place_ref, *refs,
):
    piece_refs = refs[:4]
    h_ref, skip_ref, forward_ref, back_ref, twist_ref, out_ref, drive, gate, left, right = refs[4:]
    spots = block_spots(place_ref[0])
    for spot, piece in zip(spots, piece_refs):
        for core in range(2):
            total = piece[core].astype(jnp.float32)
            for x in range(1, NX):
                total = total + piece[NC * x + core].astype(jnp.float32)
            q = 2 * spot + core
            gate[q] = total[0:32]
            drive[q] = total[32:64] * total[64:96]
    signal = [drive[q] for q in range(8)]
    for j in range(HALF_CLASSES):
        rows = slice(32 * j, 32 * j + 32)
        cos, sin = twist_ref[j, :, 0:256], twist_ref[j, :, 256:512]
        real = weighted([(small(j, q)[0], signal[q]) for q in range(8)])
        imag = weighted([(-small(j, q)[1], signal[q]) for q in range(8)])
        if imag is None:
            left[rows, 0:256] = real * cos
            left[rows, 256:512] = -real * sin
        else:
            left[rows, 0:256] = real * cos + imag * sin
            left[rows, 256:512] = imag * cos - real * sin
    right[...] = jnp.dot(
        left[...], forward_ref[...], precision=lax.Precision.HIGHEST,
        preferred_element_type=jnp.float32,
    )
    for j in range(HALF_CLASSES):
        rows = slice(32 * j, 32 * j + 32)
        h_real = h_ref[0, j].astype(jnp.float32)
        h_imag = h_ref[1, j].astype(jnp.float32)
        if 0 < j < 8:
            h_real = h_real + h_ref[0, 16 - j].astype(jnp.float32)
            h_imag = h_imag - h_ref[1, 16 - j].astype(jnp.float32)
        real, imag = right[rows, 0:256], right[rows, 256:512]
        left[rows, 0:256] = real * h_real - imag * h_imag
        left[rows, 256:512] = real * h_imag + imag * h_real
    right[...] = jnp.dot(
        left[...], back_ref[...], precision=lax.Precision.HIGHEST,
        preferred_element_type=jnp.float32,
    )
    reals, imags = [], []
    for j in range(HALF_CLASSES):
        rows = slice(32 * j, 32 * j + 32)
        cos, sin = twist_ref[j, :, 0:256], twist_ref[j, :, 256:512]
        real, imag = right[rows, 0:256], right[rows, 256:512]
        reals.append(real * cos - imag * sin)
        imags.append(real * sin + imag * cos)
    skip = skip_ref[...]
    for q in range(8):
        terms = [(small(j, q)[0], reals[j]) for j in range(HALF_CLASSES)]
        terms += [(-small(j, q)[1], imags[j]) for j in range(HALF_CLASSES)]
        convolved = weighted(terms) * (1.0 / 4096)
        out_ref[q] = (gate[q] * (convolved + skip * drive[q])).astype(out_ref.dtype)


def filtered(where, pieces, spectrum, skip):
    forward, back, twist = tables()
    vmem = pl.BlockSpec(memory_space=pltpu.VMEM)
    return pl.pallas_call(
        filter_kernel,
        out_shape=jax.ShapeDtypeStruct((8, 32, 256), jnp.bfloat16),
        in_specs=[pl.BlockSpec(memory_space=pltpu.SMEM)] + [vmem] * 9,
        out_specs=vmem,
        scratch_shapes=[
            pltpu.VMEM((8, 32, 256), jnp.float32),
            pltpu.VMEM((8, 32, 256), jnp.float32),
            pltpu.VMEM((32 * HALF_CLASSES, 512), jnp.float32),
            pltpu.VMEM((32 * HALF_CLASSES, 512), jnp.float32),
        ],
        compiler_params=pltpu.CompilerParams(vmem_limit_bytes=32 * 1024 * 1024),
    )(where, *pieces, spectrum, skip, forward, back, twist)


def spread_filter(filter_spectrum):
    first = 2 * (NC * lax.axis_index("x") + lax.axis_index("core"))
    eye = np.eye(256, dtype=np.float32)
    own = first + jnp.arange(2, dtype=jnp.int32)
    order = jnp.where((own <= 8)[:, None, None], eye[None], eye[None, :, ::-1])
    turned = jnp.einsum(
        "plgc,lgh->plch",
        filter_spectrum.astype(jnp.bfloat16),
        order.astype(jnp.bfloat16),
        preferred_element_type=jnp.float32,
    ).astype(jnp.bfloat16)
    turned = turned.reshape(2, 2, 8, 32, 256).transpose(2, 0, 1, 3, 4)
    spread = lax.all_to_all(turned, CTX, split_axis=0, concat_axis=0, tiled=True)
    return spread.transpose(1, 0, 2, 3, 4).reshape(2, 16, 32, 256)


def block_spots(z):
    own, side = z // 2, jnp.where(z % 2 == 0, -1, 1)
    return [own, (own + side) % 4, (own - side) % 4, (own + 2) % 4]


def turn_kernel(place_ref, weight_ref, out_ref):
    y = place_ref[1]
    for part in range(3):
        for k in range(4):
            block = weight_ref[part, (y + k) % 4].T
            for i in range(8):
                rows = slice(96 * i + 32 * part, 96 * i + 32 * part + 32)
                out_ref[rows, 256 * k : 256 * k + 256] = block[32 * i : 32 * i + 32]


def turned_weight(where, in_weight):
    vmem = pl.BlockSpec(memory_space=pltpu.VMEM)
    return pl.pallas_call(
        turn_kernel,
        out_shape=jax.ShapeDtypeStruct((768, 1024), jnp.bfloat16),
        in_specs=[pl.BlockSpec(memory_space=pltpu.SMEM), vmem],
        out_specs=vmem,
        compiler_params=pltpu.CompilerParams(vmem_limit_bytes=32 * 1024 * 1024),
    )(where, in_weight.reshape(3, 4, 256, 256))


def slot_kernel(steps, place_ref, *refs):
    units, (own_ref, other_ref, out_ref) = refs[:-3], refs[-3:]
    z, core = place_ref[0], place_ref[2]

    def project(unit, step):
        flip = (z + step + core) % 2
        weight = jnp.where(flip == 0, own_ref[...], other_ref[...])
        return lax.dot_general(
            weight, unit[...], (((1,), (1,)), ((), ())), preferred_element_type=jnp.float32
        )

    def put(first, second):
        total = project(first, steps[0]) + project(second, steps[1])
        out_ref[...] = total.astype(out_ref.dtype).reshape(8, 96, 256)

    if len(units) == 2:
        put(*units)
    else:
        lax.cond(z % 2 == 0, lambda: put(units[0], units[1]), lambda: put(units[2], units[3]))


def slot(where, steps, units, weights):
    vmem = pl.BlockSpec(memory_space=pltpu.VMEM)
    return pl.pallas_call(
        functools.partial(slot_kernel, steps),
        out_shape=jax.ShapeDtypeStruct((8, 96, 256), jnp.bfloat16),
        in_specs=[pl.BlockSpec(memory_space=pltpu.SMEM)] + [vmem] * (len(units) + 2),
        out_specs=vmem,
        compiler_params=pltpu.CompilerParams(vmem_limit_bytes=32 * 1024 * 1024),
    )(where, *units, *weights)


def mix_kernel(place_ref, *refs):
    blocks, weight_ref, out_ref = refs[:8], refs[8], refs[9]
    z, core = place_ref[0], place_ref[2]
    for column in range(4):
        total = jnp.zeros((256, 256), jnp.float32)
        for k in range(8):
            source = (z + k) % 8
            half = (source // 4 + core) % 2
            total += jnp.dot(
                blocks[k][...], weight_ref[half, column, source % 4],
                preferred_element_type=jnp.float32,
            )
        out_ref[column] = total.astype(out_ref.dtype)


def mix(where, blocks, weight):
    vmem = pl.BlockSpec(memory_space=pltpu.VMEM)
    return pl.pallas_call(
        mix_kernel,
        out_shape=jax.ShapeDtypeStruct((4, 256, 256), jnp.bfloat16),
        in_specs=[pl.BlockSpec(memory_space=pltpu.SMEM)] + [vmem] * 9,
        out_specs=vmem,
        compiler_params=pltpu.CompilerParams(vmem_limit_bytes=32 * 1024 * 1024),
    )(where, *blocks, weight)


def spread_weight(out_weight, core):
    halves = out_weight.reshape(2, 4, 4, 256, 256)
    own = lax.dynamic_index_in_dim(halves, core, 0, keepdims=False)
    own = lax.all_to_all(own.transpose(1, 0, 2, 3), "y", split_axis=0, concat_axis=0, tiled=True)
    return jnp.stack([own, shift(own, "core", 1)])


def shards(tokens, in_weight, filter_spectrum, skip_gain, out_weight):
    x, core = lax.axis_index("x"), lax.axis_index("core")
    z, y = lax.axis_index("z"), lax.axis_index("y")
    where = jnp.stack([z, y, core]).astype(jnp.int32)

    block = lax.ppermute(tokens, EVERY, MOVE)
    weight = turned_weight(where, in_weight)
    weights = weight, shift(weight, "core", 1)
    unit = jnp.concatenate(ring(block, "y"), 1)
    units = ring(unit, "z")
    spectrum = spread_filter(filter_spectrum)
    skip = lax.dynamic_slice_in_dim(skip_gain, 32 * (NC * x + core), 32)[:, None]
    out_weight = spread_weight(out_weight, core)
    slots = [
        ((0, 1), (units[0], units[1], units[0], units[7])),
        ((1, 2), (units[7], units[6], units[1], units[2])),
        ((2, 3), (units[2], units[3], units[6], units[5])),
        ((3, 4), (units[5], units[4], units[3], units[4])),
    ]
    pieces = [
        lax.all_to_all(
            slot(where, steps, used, weights), CTX, split_axis=0, concat_axis=0, tiled=True
        )
        for steps, used in slots
    ]
    gated = filtered(where, pieces, spectrum, skip)
    gated = lax.all_to_all(gated, CTX, split_axis=0, concat_axis=0, tiled=True)
    blocks = ring(gated.reshape(256, 256).T, "z")
    partial = mix(where, blocks, out_weight)
    parts = lax.all_to_all(partial, "y", split_axis=0, concat_axis=0, tiled=True)
    return jnp.sum(parts.astype(jnp.float32), 0).astype(jnp.bfloat16)


def solution(mesh):
    fine = Mesh(mesh.devices.reshape(NX, NC, NZ, NY), EVERY)
    tp = ("z", "y")
    placed = (P(CTX, tp), P(None, CTX, tp), P(None, CTX, None, tp), P(tp), P(None, tp))
    return jax.shard_map(
        shards, mesh=fine, in_specs=placed, out_specs=P(CTX, tp), check_vma=False
    )
```

```python
import functools
import math

import jax
import jax.numpy as jnp
import ml_dtypes
import numpy as np
from jax import lax
from jax.experimental import pallas as pl
from jax.experimental.pallas import tpu as pltpu
from jax.sharding import Mesh, PartitionSpec as P

NX, NC, NZ, NY = 4, 2, 8, 4
SIZES = dict(x=NX, core=NC, z=NZ, y=NY)
EVERY = ("x", "core", "z", "y")
CTX = ("x", "core")
HALF_CLASSES = 9


def place(x, core, z, y):
    return ((x * NC + core) * NZ + z) * NY + y


MOVE = [
    (place(p, core, 2 * x + f, y), place(x, core, 2 * p + f, y))
    for p in range(4)
    for core in range(2)
    for x in range(4)
    for f in range(2)
    for y in range(4)
]


def shift(values, axis, step):
    n = SIZES[axis]
    return lax.ppermute(values, axis, [(i, (i + step) % n) for i in range(n)])


def near_and_far(block):
    half = block.shape[0] // 2
    plus1, minus1 = shift(block, "z", -1), shift(block, "z", 1)
    plus2, minus2 = shift(block, "z", -2), shift(block, "z", 2)
    plus3, minus3 = shift(plus2, "z", -1), shift(minus2, "z", 1)
    plus4 = [shift(plus2[:half], "z", -2), shift(minus2[half:], "z", 2)]
    return [block, plus1, plus2, minus1, minus2, plus3, minus3, jnp.concatenate(plus4, 0)]


def together(*values):
    return lax.optimization_barrier(values)


@functools.lru_cache(None)
def tables():
    r = np.arange(256)
    big = 2 * np.pi * (np.outer(r, r) % 256) / 256
    c, s = np.cos(big), np.sin(big)
    both = np.concatenate([c, s], 1).astype(np.float32)
    high = both.astype(ml_dtypes.bfloat16)
    low = (both - high.astype(np.float32)).astype(ml_dtypes.bfloat16)
    j = np.arange(HALF_CLASSES)
    turn = 2 * np.pi * np.outer(j, r) / 4096
    twist = np.concatenate([np.cos(turn), np.sin(turn)], 1).astype(np.float32)
    return high, low, twist[:, None, :]


def small(j, q):
    turn = 2 * math.pi * ((j * q) % 16) / 16
    return round(math.cos(turn), 12), round(math.sin(turn), 12)


def weighted(terms):
    total = None
    for scale, value in terms:
        if scale == 0.0:
            continue
        part = value if scale == 1.0 else -value if scale == -1.0 else scale * value
        total = part if total is None else total + part
    return total


def filter_kernel(
    place_ref, *refs,
):
    (
        mine_refs, their_refs, skip_ref, sources, out_ref,
        (drive, gate, left, right, h_ref, high_ref, low_ref, twist_ref, sems),
    ) = refs[:2], refs[2:4], refs[4], refs[5:9], refs[9], refs[10:]
    tables = copy_all(zip(sources, (h_ref, high_ref, low_ref, twist_ref)), sems)

    def transform():
        for part in range(2):
            values = left[part]
            high = values.astype(jnp.bfloat16)
            low = (values - high.astype(jnp.float32)).astype(jnp.bfloat16)
            right[part] = sum(
                jnp.dot(a, b[...], preferred_element_type=jnp.float32)
                for a, b in ((high, high_ref), (high, low_ref), (low, high_ref))
            )

    z, own = place_ref[0], place_ref[2]
    for piece_refs, core in ((mine_refs, own), (their_refs, 1 - own)):
        spots = block_spots(core, z)
        for q, (index, column) in zip(spots, ((0, 0), (0, 256), (1, 0), (1, 256))):
            total = piece_refs[index][:, column : column + 256]
            gate[q] = total[0:32]
            drive[q] = total[32:64] * total[64:96]
    signal = [drive[q] for q in range(8)]
    for table in tables:
        table.wait()
    for j in range(HALF_CLASSES):
        rows = slice(32 * j, 32 * j + 32)
        cos, sin = twist_ref[j, :, 0:256], twist_ref[j, :, 256:512]
        real = weighted([(small(j, q)[0], signal[q]) for q in range(8)])
        imag = weighted([(-small(j, q)[1], signal[q]) for q in range(8)])
        if imag is None:
            left[0, rows] = real * cos
            left[1, rows] = -real * sin
        else:
            left[0, rows] = real * cos + imag * sin
            left[1, rows] = imag * cos - real * sin
    transform()
    for j in range(HALF_CLASSES):
        rows = slice(32 * j, 32 * j + 32)
        h_real = h_ref[j // 2, 0, j % 2].astype(jnp.float32)
        h_imag = h_ref[j // 2, 1, j % 2].astype(jnp.float32)
        if 0 < j < 8:
            h_real = h_real + h_ref[(16 - j) // 2, 0, j % 2].astype(jnp.float32)
            h_imag = h_imag - h_ref[(16 - j) // 2, 1, j % 2].astype(jnp.float32)
        real = right[0, rows, 0:256] + right[1, rows, 256:512]
        imag = right[1, rows, 0:256] - right[0, rows, 256:512]
        left[0, rows] = real * h_real - imag * h_imag
        left[1, rows] = real * h_imag + imag * h_real
    transform()
    reals, imags = [], []
    for j in range(HALF_CLASSES):
        rows = slice(32 * j, 32 * j + 32)
        cos, sin = twist_ref[j, :, 0:256], twist_ref[j, :, 256:512]
        real = right[0, rows, 0:256] - right[1, rows, 256:512]
        imag = right[1, rows, 0:256] + right[0, rows, 256:512]
        reals.append(real * cos - imag * sin)
        imags.append(real * sin + imag * cos)
    skip = skip_ref[...]
    for q in range(8):
        terms = [(small(j, q)[0], reals[j]) for j in range(HALF_CLASSES)]
        terms += [(-small(j, q)[1], imags[j]) for j in range(HALF_CLASSES)]
        convolved = weighted(terms) * (1.0 / 4096)
        out_ref[q] = (gate[q] * (convolved + skip * drive[q])).astype(out_ref.dtype)


def filtered(where, pieces, spectrum, skip):
    high, low, twist = tables()
    vmem = pl.BlockSpec(memory_space=pltpu.VMEM)
    return pl.pallas_call(
        filter_kernel,
        out_shape=jax.ShapeDtypeStruct((8, 32, 256), jnp.bfloat16),
        in_specs=[pl.BlockSpec(memory_space=pltpu.SMEM)]
        + [vmem] * 5
        + [pl.BlockSpec(memory_space=pl.ANY)] * 4,
        out_specs=vmem,
        scratch_shapes=[
            pltpu.VMEM((8, 32, 256), jnp.float32),
            pltpu.VMEM((8, 32, 256), jnp.float32),
            pltpu.VMEM((2, 32 * HALF_CLASSES, 256), jnp.float32),
            pltpu.VMEM((2, 32 * HALF_CLASSES, 512), jnp.float32),
            pltpu.VMEM((8, 2, 2, 32, 256), jnp.bfloat16),
            pltpu.VMEM((256, 512), jnp.bfloat16),
            pltpu.VMEM((256, 512), jnp.bfloat16),
            pltpu.VMEM((HALF_CLASSES, 1, 512), jnp.float32),
            pltpu.SemaphoreType.DMA((4,)),
        ],
        compiler_params=pltpu.CompilerParams(vmem_limit_bytes=16 * 1024 * 1024),
        cost_estimate=cost(3),
    )(where, *pieces, skip, spectrum, high, low, twist)


def turned_filter(filter_spectrum):
    first = 2 * (NC * lax.axis_index("x") + lax.axis_index("core"))
    eye = np.eye(256, dtype=np.float32)
    own = first + jnp.arange(2, dtype=jnp.int32)
    order = jnp.where((own <= 8)[:, None, None], eye[None], eye[None, :, ::-1])
    turned = jnp.einsum(
        "plgc,lgh->plch",
        filter_spectrum.astype(jnp.bfloat16),
        order.astype(jnp.bfloat16),
        preferred_element_type=jnp.float32,
    ).astype(jnp.bfloat16)
    return turned.reshape(2, 2, 8, 32, 256).transpose(2, 0, 1, 3, 4)


def block_spots(core, z):
    side = jnp.where(z % 2 == 0, 3, 1)
    quarters = [z // 2, z // 2 + side, z // 2 + 4 - side, z // 2 + 2]
    return [2 * (quarter % 4) + core for quarter in quarters]


def cost(microseconds):
    return pl.CostEstimate(
        flops=int(microseconds * 1e9), bytes_accessed=int(microseconds * 3e6), transcendentals=0
    )


def turn_kernel(place_ref, own_ref, sibling_ref, hbm_ref, turned, out_ref, sems):
    z, y, core, x = (place_ref[i] for i in range(4))

    def turn(piece, feature, y_at):
        def put(ref):
            for part in range(3):
                turned[part] = ref[part, y_at].T

        pl.when(feature == core)(lambda: put(own_ref))
        pl.when(feature != core)(lambda: put(sibling_ref))
        columns = slice(256 * (piece % 4), 256 * (piece % 4) + 256)
        for k in range(4):
            for side in range(2):
                start = pl.multiple_of(32 * (2 * ((x + k) % 4) + (core + side) % 2), 32)
                for part in range(3):
                    row = 192 * k + 96 * side + 32 * part
                    out_ref[piece // 4, row : row + 32, columns] = turned[part, pl.ds(start, 32)]

    copies = []
    for half in range(2):
        for piece in range(4 * half, 4 * half + 4):
            turn(piece, (z + half) % 2, (y + piece) % 4)
        copies += copy_all([(out_ref.at[half], hbm_ref.at[half])], sems.at[pl.ds(half, 1)])
    for copy in copies:
        copy.wait()


def turned_weight(where, own, sibling):
    vmem = pl.BlockSpec(memory_space=pltpu.VMEM)
    return pl.pallas_call(
        turn_kernel,
        out_shape=jax.ShapeDtypeStruct((2, 768, 1024), jnp.bfloat16),
        in_specs=[pl.BlockSpec(memory_space=pltpu.SMEM), vmem, vmem],
        out_specs=pl.BlockSpec(memory_space=pltpu.HBM),
        scratch_shapes=[
            pltpu.VMEM((3, 256, 256), jnp.bfloat16),
            pltpu.VMEM((2, 768, 1024), jnp.bfloat16),
            pltpu.SemaphoreType.DMA((2,)),
        ],
        compiler_params=pltpu.CompilerParams(vmem_limit_bytes=16 * 1024 * 1024),
        cost_estimate=cost(3),
    )(where, own.reshape(3, 4, 256, 256), sibling.reshape(3, 4, 256, 256))


def copy_all(pairs, sems):
    copies = [
        pltpu.make_async_copy(source, target, sems.at[index])
        for index, (source, target) in enumerate(pairs)
    ]
    for copy in copies:
        copy.start()
    return copies


def join_kernel(*refs):
    parts, out_refs = refs[:4], refs[4:6]
    for k, part in enumerate(parts):
        for half, out_ref in enumerate(out_refs):
            out_ref[:, 256 * k : 256 * k + 256] = part[128 * half : 128 * half + 128]


def joined(parts):
    vmem = pl.BlockSpec(memory_space=pltpu.VMEM)
    return pl.pallas_call(
        join_kernel,
        out_shape=[jax.ShapeDtypeStruct((128, 1024), jnp.bfloat16)] * 2,
        in_specs=[vmem] * 4,
        out_specs=[vmem] * 2,
        cost_estimate=cost(2),
    )(*parts)


def slot_kernel(blocks, count, place_ref, *refs):
    sources, out_refs = refs[: 2 * count + 1], refs[2 * count + 1 : 2 * count + 5]
    unit_ref, weight_ref, sems = refs[2 * count + 5 :]
    pairs = [
        (sources[index], unit_ref.at[index // 2, pl.ds(128 * (index % 2), 128)])
        for index in range(2 * count)
    ]
    copies = copy_all(pairs + [(sources[-1], weight_ref)], sems)
    for copy in copies:
        copy.wait()

    def run(case):
        for index, block in enumerate(blocks):
            total = sum(
                lax.dot_general(
                    weight_ref[half], unit_ref[unit], (((1,), (1,)), ((), ())),
                    preferred_element_type=jnp.float32,
                )
                for unit, half in block[case]
            )
            columns = slice(256 * index, 256 * index + 256)
            for k, out_ref in enumerate(out_refs):
                rows = slice(192 * k, 192 * k + 192)
                out_ref[:, columns] = total[rows].astype(out_ref.dtype)

    for number in range(2):
        pl.when(place_ref[0] % 2 == number)(functools.partial(run, number))


def slot(where, units, weight, *blocks):
    names = sorted({name for block in blocks for case in block for name, _ in case})
    order = {name: index for index, name in enumerate(names)}
    blocks = [[[(order[name], half) for name, half in case] for case in block] for block in blocks]
    vmem = pl.BlockSpec(memory_space=pltpu.VMEM)
    anywhere = pl.BlockSpec(memory_space=pl.ANY)
    shape = (192, 256 * len(blocks))
    return pl.pallas_call(
        functools.partial(slot_kernel, blocks, len(names)),
        out_shape=[jax.ShapeDtypeStruct(shape, jnp.float32)]
        + [jax.ShapeDtypeStruct(shape, jnp.bfloat16)] * 3,
        in_specs=[pl.BlockSpec(memory_space=pltpu.SMEM)]
        + [anywhere] * (2 * len(names))
        + [pl.BlockSpec(memory_space=pltpu.HBM)],
        out_specs=[vmem] * 4,
        scratch_shapes=[
            pltpu.VMEM((len(names), 256, 1024), jnp.bfloat16),
            pltpu.VMEM((2, 768, 1024), jnp.bfloat16),
            pltpu.SemaphoreType.DMA((2 * len(names) + 1,)),
        ],
        compiler_params=pltpu.CompilerParams(vmem_limit_bytes=16 * 1024 * 1024),
        cost_estimate=cost(3),
    )(where, *[half for name in names for half in units[name]], weight)


def sum_over_x(parts):
    total = parts[0]
    for k in (1, 2, 3):
        total = total + shift(parts[k], "x", k).astype(jnp.float32)
    return total[:96], shift(total[96:], "core", 1)


def mix_kernel(place_ref, *refs):
    blocks, weights, out_ref, ordered = refs[:8], refs[8:10], refs[10], refs[11]
    z, core = place_ref[0], place_ref[2]
    for k, step in enumerate((0, 1, 2, 7, 6, 3, 5, 4)):
        ordered[(z + step + 4 * core) % 8] = blocks[k][...]
    for column in range(4):
        total = sum(
            jnp.dot(
                ordered[4 * side + row], weights[side][column, row],
                preferred_element_type=jnp.float32,
            )
            for side in range(2)
            for row in range(4)
        )
        out_ref[column] = total.astype(out_ref.dtype)


def mix(where, blocks, weights):
    vmem = pl.BlockSpec(memory_space=pltpu.VMEM)
    return pl.pallas_call(
        mix_kernel,
        out_shape=jax.ShapeDtypeStruct((4, 256, 256), jnp.bfloat16),
        in_specs=[pl.BlockSpec(memory_space=pltpu.SMEM)] + [vmem] * 10,
        out_specs=vmem,
        scratch_shapes=[pltpu.VMEM((8, 256, 256), jnp.bfloat16)],
        compiler_params=pltpu.CompilerParams(vmem_limit_bytes=16 * 1024 * 1024),
        cost_estimate=cost(2),
    )(where, *blocks, *weights)


def over_ctx(values):
    return lax.all_to_all(values, CTX, split_axis=0, concat_axis=0, tiled=True)


def shards(tokens, in_weight, filter_spectrum, skip_gain, out_weight):
    x, core = lax.axis_index("x"), lax.axis_index("core")
    z, y = lax.axis_index("z"), lax.axis_index("y")
    where = jnp.stack([z, y, core, x]).astype(jnp.int32)

    block = lax.ppermute(tokens, EVERY, MOVE)
    sibling = shift(in_weight, "core", 1)
    sent_filter = turned_filter(filter_spectrum)
    skip = lax.dynamic_slice_in_dim(skip_gain, 32 * (NC * x + core), 32)[:, None]
    mine = lax.dynamic_index_in_dim(
        out_weight.reshape(2, 4, 4, 256, 256), core, 0, keepdims=False
    )
    rows = [
        lax.dynamic_index_in_dim(mine, (y + 4 - k) % 4, 1, keepdims=False) for k in range(4)
    ]
    block, rows = together(block, rows)

    spectrum = over_ctx(sent_filter)
    halves = joined([block] + [shift(block, "y", -k) for k in (1, 2, 3)])
    spectrum, halves, rows = together(spectrum, halves, rows)
    units = {"own": halves}
    up, down = ([shift(half, "z", step) for half in halves] for step in (1, -1))
    units["up1"], units["down1"] = up, down
    rows[1] = shift(rows[1], "y", -1)

    weight = turned_weight(where, in_weight, sibling)
    weight, rows, last = together(weight, rows, [up[1], down[1]])
    up, down = (
        [shift(first, "z", step), shift(second, "z", step)]
        for first, second, step in ((up[0], last[0], 1), (down[0], last[1], -1))
    )
    units["up2"], units["down2"] = up, down
    rows[3] = shift(rows[3], "y", -3)

    rows, last = together(rows, [up[1], down[1]])
    up, down = (
        [shift(first, "z", step), shift(second, "z", step)]
        for first, second, step in ((up[0], last[0], 1), (down[0], last[1], -1))
    )
    units["up3"], units["down3"] = up, down
    rows[2] = shift(rows[2], "y", -2)
    parts = slot(
        where, units, weight,
        [[("own", 0), ("down1", 1)], [("own", 0), ("up1", 1)]],
        [[("up1", 1), ("up2", 0)], [("down1", 1), ("down2", 0)]],
    )
    parts, last = together(parts, down[1])
    pieces = [sum_over_x(parts)]

    units["across"] = [shift(up[0], "z", 1), shift(last, "z", -1)]
    pieces[0], units["across"] = together(pieces[0], units["across"])
    parts = slot(
        where, units, weight,
        [[("down2", 0), ("down3", 1)], [("up2", 0), ("up3", 1)]],
        [[("up3", 1), ("across", 0)], [("down3", 1), ("across", 0)]],
    )
    pieces.append(sum_over_x(parts))
    pieces = [piece[0] for piece in pieces] + [piece[1] for piece in pieces]
    pieces, rows = together(pieces, rows)
    rows = jnp.stack(rows)

    gated = filtered(where, pieces, spectrum, skip)
    gated = over_ctx(gated).reshape(256, 256).T
    partial = mix(where, near_and_far(gated), [rows, shift(rows, "core", 1)])
    total = partial[0].astype(jnp.float32)
    for k in (1, 2, 3):
        total = total + shift(partial[k], "y", k).astype(jnp.float32)
    return total.astype(jnp.bfloat16)


def solution(mesh):
    fine = Mesh(mesh.devices.reshape(NX, NC, NZ, NY), EVERY)
    tp = ("z", "y")
    placed = (P(CTX, tp), P(None, CTX, tp), P(None, CTX, None, tp), P(tp), P(None, tp))
    return jax.shard_map(
        shards, mesh=fine, in_specs=placed, out_specs=P(CTX, tp), check_vma=False
    )
```

```python
import functools
import math

import jax
import jax.numpy as jnp
import ml_dtypes
import numpy as np
from jax import lax
from jax.experimental import pallas as pl
from jax.experimental.pallas import tpu as pltpu
from jax.sharding import Mesh, PartitionSpec as P

NX, NC, NZ, NY = 4, 2, 8, 4
SIZES = dict(x=NX, core=NC, z=NZ, y=NY)
EVERY = ("x", "core", "z", "y")
CTX = ("x", "core")
HALF_CLASSES = 9


def place(x, core, z, y):
    return ((x * NC + core) * NZ + z) * NY + y


MOVE = [
    (place(p, core, 2 * x + f, y), place(x, core, 2 * p + f, y))
    for p in range(4)
    for core in range(2)
    for x in range(4)
    for f in range(2)
    for y in range(4)
]


def shift(values, axis, step):
    n = SIZES[axis]
    return lax.ppermute(values, axis, [(i, (i + step) % n) for i in range(n)])


def near_and_far(block):
    half = block.shape[0] // 2
    plus1, minus1 = shift(block, "z", -1), shift(block, "z", 1)
    plus2, minus2 = shift(block, "z", -2), shift(block, "z", 2)
    plus1, minus1, plus2, minus2 = together(plus1, minus1, plus2, minus2)
    plus3, minus3 = shift(plus2, "z", -1), shift(minus2, "z", 1)
    plus4 = [shift(plus2[:half], "z", -2), shift(minus2[half:], "z", 2)]
    return [block, plus1, plus2, minus1, minus2, plus3, minus3, jnp.concatenate(plus4, 0)]


def together(*values):
    return lax.optimization_barrier(values)


@functools.lru_cache(None)
def tables():
    r = np.arange(256)
    big = 2 * np.pi * (np.outer(r, r) % 256) / 256
    c, s = np.cos(big), np.sin(big)
    both = np.concatenate([c, s], 1).astype(np.float32)
    high = both.astype(ml_dtypes.bfloat16)
    low = (both - high.astype(np.float32)).astype(ml_dtypes.bfloat16)
    j = np.arange(HALF_CLASSES)
    turn = 2 * np.pi * np.outer(j, r) / 4096
    twist = np.concatenate([np.cos(turn), np.sin(turn)], 1).astype(np.float32)
    return high, low, twist[:, None, :]


def small(j, q):
    turn = 2 * math.pi * ((j * q) % 16) / 16
    return round(math.cos(turn), 12), round(math.sin(turn), 12)


def weighted(terms):
    total = None
    for scale, value in terms:
        if scale == 0.0:
            continue
        part = value if scale == 1.0 else -value if scale == -1.0 else scale * value
        total = part if total is None else total + part
    return total


def filter_kernel(
    place_ref, *refs,
):
    (
        skip_ref, sources, out_ref,
        (drive, gate, left, right, h_ref, high_ref, low_ref, twist_ref, piece_ref, sems),
    ) = refs[0], refs[1:9], refs[9], refs[10:]
    targets = [piece_ref.at[k] for k in range(4)] + [h_ref, high_ref, low_ref, twist_ref]
    copies = copy_all(zip(sources, targets), sems)
    tables = copies[4:]
    for copy in copies[:4]:
        copy.wait()

    def transform():
        for part in range(2):
            values = left[part]
            high = values.astype(jnp.bfloat16)
            low = (values - high.astype(jnp.float32)).astype(jnp.bfloat16)
            right[part] = sum(
                jnp.dot(a, b[...], preferred_element_type=jnp.float32)
                for a, b in ((high, high_ref), (high, low_ref), (low, high_ref))
            )

    z, own = place_ref[0], place_ref[2]
    for side, core in enumerate((own, 1 - own)):
        spots = block_spots(core, z)
        for q, (index, column) in zip(spots, ((0, 0), (0, 256), (1, 0), (1, 256))):
            total = piece_ref[2 * side + index, :, column : column + 256]
            gate[q] = total[0:32]
            drive[q] = total[32:64] * total[64:96]
    signal = [drive[q] for q in range(8)]
    for table in tables:
        table.wait()
    for j in range(HALF_CLASSES):
        rows = slice(32 * j, 32 * j + 32)
        cos, sin = twist_ref[j, :, 0:256], twist_ref[j, :, 256:512]
        real = weighted([(small(j, q)[0], signal[q]) for q in range(8)])
        imag = weighted([(-small(j, q)[1], signal[q]) for q in range(8)])
        if imag is None:
            left[0, rows] = real * cos
            left[1, rows] = -real * sin
        else:
            left[0, rows] = real * cos + imag * sin
            left[1, rows] = imag * cos - real * sin
    transform()
    for j in range(HALF_CLASSES):
        rows = slice(32 * j, 32 * j + 32)
        h_real = h_ref[j // 2, 0, j % 2].astype(jnp.float32)
        h_imag = h_ref[j // 2, 1, j % 2].astype(jnp.float32)
        if 0 < j < 8:
            h_real = h_real + h_ref[(16 - j) // 2, 0, j % 2].astype(jnp.float32)
            h_imag = h_imag - h_ref[(16 - j) // 2, 1, j % 2].astype(jnp.float32)
        real = right[0, rows, 0:256] + right[1, rows, 256:512]
        imag = right[1, rows, 0:256] - right[0, rows, 256:512]
        left[0, rows] = real * h_real - imag * h_imag
        left[1, rows] = real * h_imag + imag * h_real
    transform()
    reals, imags = [], []
    for j in range(HALF_CLASSES):
        rows = slice(32 * j, 32 * j + 32)
        cos, sin = twist_ref[j, :, 0:256], twist_ref[j, :, 256:512]
        real = right[0, rows, 0:256] - right[1, rows, 256:512]
        imag = right[1, rows, 0:256] + right[0, rows, 256:512]
        reals.append(real * cos - imag * sin)
        imags.append(real * sin + imag * cos)
    skip = skip_ref[...]
    for q in range(8):
        terms = [(small(j, q)[0], reals[j]) for j in range(HALF_CLASSES)]
        terms += [(-small(j, q)[1], imags[j]) for j in range(HALF_CLASSES)]
        convolved = weighted(terms) * (1.0 / 4096)
        out_ref[q] = (gate[q] * (convolved + skip * drive[q])).astype(out_ref.dtype)


def filtered(where, pieces, spectrum, skip):
    high, low, twist = tables()
    vmem = pl.BlockSpec(memory_space=pltpu.VMEM)
    return pl.pallas_call(
        filter_kernel,
        out_shape=jax.ShapeDtypeStruct((8, 32, 256), jnp.bfloat16),
        in_specs=[pl.BlockSpec(memory_space=pltpu.SMEM)]
        + [vmem]
        + [pl.BlockSpec(memory_space=pl.ANY)] * 8,
        out_specs=vmem,
        scratch_shapes=[
            pltpu.VMEM((8, 32, 256), jnp.float32),
            pltpu.VMEM((8, 32, 256), jnp.float32),
            pltpu.VMEM((2, 32 * HALF_CLASSES, 256), jnp.float32),
            pltpu.VMEM((2, 32 * HALF_CLASSES, 512), jnp.float32),
            pltpu.VMEM((8, 2, 2, 32, 256), jnp.bfloat16),
            pltpu.VMEM((256, 512), jnp.bfloat16),
            pltpu.VMEM((256, 512), jnp.bfloat16),
            pltpu.VMEM((HALF_CLASSES, 1, 512), jnp.float32),
            pltpu.VMEM((4, 96, 512), jnp.float32),
            pltpu.SemaphoreType.DMA((8,)),
        ],
        compiler_params=pltpu.CompilerParams(vmem_limit_bytes=16 * 1024 * 1024),
        cost_estimate=cost(3),
    )(where, skip, *pieces, spectrum, high, low, twist)


def turned_filter(filter_spectrum):
    first = 2 * (NC * lax.axis_index("x") + lax.axis_index("core"))
    eye = np.eye(256, dtype=np.float32)
    own = first + jnp.arange(2, dtype=jnp.int32)
    order = jnp.where((own <= 8)[:, None, None], eye[None], eye[None, :, ::-1])
    turned = jnp.einsum(
        "plgc,lgh->plch",
        filter_spectrum.astype(jnp.bfloat16),
        order.astype(jnp.bfloat16),
        preferred_element_type=jnp.float32,
    ).astype(jnp.bfloat16)
    return turned.reshape(2, 2, 8, 32, 256).transpose(2, 0, 1, 3, 4)


def block_spots(core, z):
    side = jnp.where(z % 2 == 0, 3, 1)
    quarters = [z // 2, z // 2 + side, z // 2 + 4 - side, z // 2 + 2]
    return [2 * (quarter % 4) + core for quarter in quarters]


def cost(microseconds):
    return pl.CostEstimate(
        flops=int(microseconds * 1e9), bytes_accessed=int(microseconds * 3e6), transcendentals=0
    )


def turn_kernel(place_ref, own_ref, sibling_ref, hbm_ref, turned, out_ref, sems):
    z, y, core, x = (place_ref[i] for i in range(4))

    def turn(piece, feature, y_at):
        def put(ref):
            for part in range(3):
                turned[part] = ref[part, y_at].T

        pl.when(feature == core)(lambda: put(own_ref))
        pl.when(feature != core)(lambda: put(sibling_ref))
        columns = slice(256 * (piece % 4), 256 * (piece % 4) + 256)
        for k in range(4):
            for side in range(2):
                start = pl.multiple_of(32 * (2 * ((x + k) % 4) + (core + side) % 2), 32)
                for part in range(3):
                    row = 192 * k + 96 * side + 32 * part
                    out_ref[piece // 4, row : row + 32, columns] = turned[part, pl.ds(start, 32)]

    copies = []
    for half in range(2):
        for piece in range(4 * half, 4 * half + 4):
            turn(piece, (z + half) % 2, (y + piece) % 4)
        copies += copy_all([(out_ref.at[half], hbm_ref.at[half])], sems.at[pl.ds(half, 1)])
    for copy in copies:
        copy.wait()


def turned_weight(where, own, sibling):
    vmem = pl.BlockSpec(memory_space=pltpu.VMEM)
    return pl.pallas_call(
        turn_kernel,
        out_shape=jax.ShapeDtypeStruct((2, 768, 1024), jnp.bfloat16),
        in_specs=[pl.BlockSpec(memory_space=pltpu.SMEM), vmem, vmem],
        out_specs=pl.BlockSpec(memory_space=pltpu.HBM),
        scratch_shapes=[
            pltpu.VMEM((3, 256, 256), jnp.bfloat16),
            pltpu.VMEM((2, 768, 1024), jnp.bfloat16),
            pltpu.SemaphoreType.DMA((2,)),
        ],
        compiler_params=pltpu.CompilerParams(vmem_limit_bytes=16 * 1024 * 1024),
        cost_estimate=cost(3),
    )(where, own.reshape(3, 4, 256, 256), sibling.reshape(3, 4, 256, 256))


def copy_all(pairs, sems):
    copies = [
        pltpu.make_async_copy(source, target, sems.at[index])
        for index, (source, target) in enumerate(pairs)
    ]
    for copy in copies:
        copy.start()
    return copies


def join_kernel(*refs):
    parts, out_refs = refs[:4], refs[4:6]
    for k, part in enumerate(parts):
        for half, out_ref in enumerate(out_refs):
            out_ref[:, 256 * k : 256 * k + 256] = part[128 * half : 128 * half + 128]


def joined(parts):
    vmem = pl.BlockSpec(memory_space=pltpu.VMEM)
    return pl.pallas_call(
        join_kernel,
        out_shape=[jax.ShapeDtypeStruct((128, 1024), jnp.bfloat16)] * 2,
        in_specs=[vmem] * 4,
        out_specs=[vmem] * 2,
        cost_estimate=cost(2),
    )(*parts)


def slot_kernel(blocks, count, place_ref, *refs):
    sources, out_refs = refs[: 2 * count + 1], refs[2 * count + 1 : 2 * count + 5]
    unit_ref, weight_ref, sems = refs[2 * count + 5 :]
    pairs = [
        (sources[index], unit_ref.at[index // 2, pl.ds(128 * (index % 2), 128)])
        for index in range(2 * count)
    ]
    copies = copy_all(pairs + [(sources[-1], weight_ref)], sems)
    for copy in copies:
        copy.wait()

    def run(case):
        for index, block in enumerate(blocks):
            total = sum(
                lax.dot_general(
                    weight_ref[half], unit_ref[unit], (((1,), (1,)), ((), ())),
                    preferred_element_type=jnp.float32,
                )
                for unit, half in block[case]
            )
            columns = slice(256 * index, 256 * index + 256)
            for k, out_ref in enumerate(out_refs):
                rows = slice(192 * k, 192 * k + 192)
                out_ref[:, columns] = total[rows].astype(out_ref.dtype)

    for number in range(2):
        pl.when(place_ref[0] % 2 == number)(functools.partial(run, number))


def slot(where, units, weight, *blocks):
    names = sorted({name for block in blocks for case in block for name, _ in case})
    order = {name: index for index, name in enumerate(names)}
    blocks = [[[(order[name], half) for name, half in case] for case in block] for block in blocks]
    vmem = pl.BlockSpec(memory_space=pltpu.VMEM)
    anywhere = pl.BlockSpec(memory_space=pl.ANY)
    shape = (192, 256 * len(blocks))
    return pl.pallas_call(
        functools.partial(slot_kernel, blocks, len(names)),
        out_shape=[jax.ShapeDtypeStruct(shape, jnp.float32)]
        + [jax.ShapeDtypeStruct(shape, jnp.bfloat16)] * 3,
        in_specs=[pl.BlockSpec(memory_space=pltpu.SMEM)]
        + [anywhere] * (2 * len(names))
        + [pl.BlockSpec(memory_space=pltpu.HBM)],
        out_specs=[vmem] * 4,
        scratch_shapes=[
            pltpu.VMEM((len(names), 256, 1024), jnp.bfloat16),
            pltpu.VMEM((2, 768, 1024), jnp.bfloat16),
            pltpu.SemaphoreType.DMA((2 * len(names) + 1,)),
        ],
        compiler_params=pltpu.CompilerParams(vmem_limit_bytes=16 * 1024 * 1024),
        cost_estimate=cost(3),
    )(where, *[half for name in names for half in units[name]], weight)


def sum_over_x(parts):
    total = parts[0]
    for k in (1, 2, 3):
        total = total + shift(parts[k], "x", k).astype(jnp.float32)
    return total[:96], shift(total[96:], "core", 1)


def mix_kernel(place_ref, *refs):
    blocks, weights, out_ref, ordered = refs[:8], refs[8:10], refs[10], refs[11]
    z, core = place_ref[0], place_ref[2]
    for k, step in enumerate((0, 1, 2, 7, 6, 3, 5, 4)):
        ordered[(z + step + 4 * core) % 8] = blocks[k][...]
    for column in range(4):
        total = sum(
            jnp.dot(
                ordered[4 * side + row], weights[side][column, row],
                preferred_element_type=jnp.float32,
            )
            for side in range(2)
            for row in range(4)
        )
        out_ref[column] = total.astype(out_ref.dtype)


def mix(where, blocks, weights):
    vmem = pl.BlockSpec(memory_space=pltpu.VMEM)
    return pl.pallas_call(
        mix_kernel,
        out_shape=jax.ShapeDtypeStruct((4, 256, 256), jnp.bfloat16),
        in_specs=[pl.BlockSpec(memory_space=pltpu.SMEM)] + [vmem] * 10,
        out_specs=vmem,
        scratch_shapes=[pltpu.VMEM((8, 256, 256), jnp.bfloat16)],
        compiler_params=pltpu.CompilerParams(vmem_limit_bytes=16 * 1024 * 1024),
        cost_estimate=cost(2),
    )(where, *blocks, *weights)


def over_ctx(values):
    return lax.all_to_all(values, CTX, split_axis=0, concat_axis=0, tiled=True)


def shards(tokens, in_weight, filter_spectrum, skip_gain, out_weight):
    x, core = lax.axis_index("x"), lax.axis_index("core")
    z, y = lax.axis_index("z"), lax.axis_index("y")
    where = jnp.stack([z, y, core, x]).astype(jnp.int32)

    block = lax.ppermute(tokens, EVERY, MOVE)
    sibling = shift(in_weight, "core", 1)
    sent_filter = turned_filter(filter_spectrum)
    skip = lax.dynamic_slice_in_dim(skip_gain, 32 * (NC * x + core), 32)[:, None]
    spectrum = over_ctx(sent_filter)
    blocks = [block] + [shift(block, "y", -k) for k in (1, 2, 3)]

    out_weight, _ = together(out_weight, block)
    mine = lax.dynamic_index_in_dim(
        out_weight.reshape(2, 4, 4, 256, 256), core, 0, keepdims=False
    )
    rows = [
        lax.dynamic_index_in_dim(mine, (y + 4 - k) % 4, 1, keepdims=False) for k in range(4)
    ]
    halves = joined(blocks)
    spectrum, halves, rows = together(spectrum, halves, rows)
    units = {"own": halves}
    up, down = ([shift(half, "z", step) for half in halves] for step in (1, -1))
    units["up1"], units["down1"] = up, down
    rows[1] = shift(rows[1], "y", -1)

    weight = turned_weight(where, in_weight, sibling)
    weight, last = together(weight, [up[1], down[1]])
    up, down = (
        [shift(first, "z", step), shift(second, "z", step)]
        for first, second, step in ((up[0], last[0], 1), (down[0], last[1], -1))
    )
    units["up2"], units["down2"] = up, down

    rows[1], rows[3], last = together(rows[1], rows[3], [up[1], down[1]])
    rows[3] = shift(rows[3], "y", -3)
    up, down = (
        [shift(first, "z", step), shift(second, "z", step)]
        for first, second, step in ((up[0], last[0], 1), (down[0], last[1], -1))
    )
    units["up3"], units["down3"] = up, down
    parts = slot(
        where, units, weight,
        [[("own", 0), ("down1", 1)], [("own", 0), ("up1", 1)]],
        [[("up1", 1), ("up2", 0)], [("down1", 1), ("down2", 0)]],
    )
    parts, rows[3], last = together(parts, rows[3], down[1])
    pieces = [sum_over_x(parts)]

    units["across"] = [shift(up[0], "z", 1), shift(last, "z", -1)]
    pieces[0], units["across"] = together(pieces[0], units["across"])
    parts = slot(
        where, units, weight,
        [[("down2", 0), ("down3", 1)], [("up2", 0), ("up3", 1)]],
        [[("up3", 1), ("across", 0)], [("down3", 1), ("across", 0)]],
    )
    rows[2], _ = together(rows[2], parts[0])
    rows[2] = shift(rows[2], "y", -2)
    pieces.append(sum_over_x(parts))
    pieces = [piece[0] for piece in pieces] + [piece[1] for piece in pieces]

    gated = filtered(where, pieces, spectrum, skip)
    gated = over_ctx(gated).reshape(256, 256).T
    rows, _ = together(rows, gated)
    rows = jnp.stack(rows)
    partial = mix(where, near_and_far(gated), [rows, shift(rows, "core", 1)])
    total = partial[0].astype(jnp.float32)
    for k in (1, 2, 3):
        total = total + shift(partial[k], "y", k).astype(jnp.float32)
    return total.astype(jnp.bfloat16)


def solution(mesh):
    fine = Mesh(mesh.devices.reshape(NX, NC, NZ, NY), EVERY)
    tp = ("z", "y")
    placed = (P(CTX, tp), P(None, CTX, tp), P(None, CTX, None, tp), P(tp), P(None, tp))
    return jax.shard_map(
        shards, mesh=fine, in_specs=placed, out_specs=P(CTX, tp), check_vma=False
    )
```

```python
import functools
import math

import jax
import jax.numpy as jnp
import ml_dtypes
import numpy as np
from jax import lax
from jax.experimental import pallas as pl
from jax.experimental.pallas import tpu as pltpu
from jax.sharding import Mesh, PartitionSpec as P

NX, NC, NZ, NY = 4, 2, 8, 4
SIZES = dict(x=NX, core=NC, z=NZ, y=NY)
EVERY = ("x", "core", "z", "y")
CTX = ("x", "core")
HALF_CLASSES = 9


def place(x, core, z, y):
    return ((x * NC + core) * NZ + z) * NY + y


MOVE = [
    (place(p, core, 2 * x + f, y), place(x, core, 2 * p + f, y))
    for p in range(4)
    for core in range(2)
    for x in range(4)
    for f in range(2)
    for y in range(4)
]


def shift(values, axis, step):
    n = SIZES[axis]
    return lax.ppermute(values, axis, [(i, (i + step) % n) for i in range(n)])


def near_z(block):
    return together(
        shift(block, "z", -2), shift(block, "z", 2), shift(block, "z", -1), shift(block, "z", 1)
    )


def far_z(plus2, minus2):
    half = plus2.shape[0] // 2
    plus4 = [shift(plus2[:half], "z", -2), shift(minus2[half:], "z", 2)]
    return [shift(plus2, "z", -1), shift(minus2, "z", 1), jnp.concatenate(plus4, 0)]


def together(*values):
    return lax.optimization_barrier(values)


@functools.lru_cache(None)
def tables():
    r = np.arange(256)
    big = 2 * np.pi * (np.outer(r, r) % 256) / 256
    c, s = np.cos(big), np.sin(big)
    both = np.concatenate([c, s], 1).astype(np.float32)
    high = both.astype(ml_dtypes.bfloat16)
    low = (both - high.astype(np.float32)).astype(ml_dtypes.bfloat16)
    j = np.arange(HALF_CLASSES)
    turn = 2 * np.pi * np.outer(j, r) / 4096
    twist = np.concatenate([np.cos(turn), np.sin(turn)], 1).astype(np.float32)
    return high, low, twist[:, None, :]


def small(j, q):
    turn = 2 * math.pi * ((j * q) % 16) / 16
    return round(math.cos(turn), 12), round(math.sin(turn), 12)


def weighted(terms):
    total = None
    for scale, value in terms:
        if scale == 0.0:
            continue
        part = value if scale == 1.0 else -value if scale == -1.0 else scale * value
        total = part if total is None else total + part
    return total


def filter_kernel(
    place_ref, *refs,
):
    (
        skip_ref, sources, out_ref,
        (drive, gate, left, right, h_ref, high_ref, low_ref, twist_ref, piece_ref, sems),
    ) = refs[0], refs[1:9], refs[9], refs[10:]
    targets = [piece_ref.at[k] for k in range(4)] + [h_ref, high_ref, low_ref, twist_ref]
    copies = copy_all(zip(sources, targets), sems)
    tables = copies[4:]
    for copy in copies[:4]:
        copy.wait()

    def transform():
        for part in range(2):
            values = left[part]
            high = values.astype(jnp.bfloat16)
            low = (values - high.astype(jnp.float32)).astype(jnp.bfloat16)
            right[part] = sum(
                jnp.dot(a, b[...], preferred_element_type=jnp.float32)
                for a, b in ((high, high_ref), (high, low_ref), (low, high_ref))
            )

    z, own = place_ref[0], place_ref[2]
    for side, core in enumerate((own, 1 - own)):
        spots = block_spots(core, z)
        for q, (index, column) in zip(spots, ((0, 0), (0, 256), (1, 0), (1, 256))):
            total = piece_ref[2 * side + index, :, column : column + 256]
            gate[q] = total[0:32]
            drive[q] = total[32:64] * total[64:96]
    signal = [drive[q] for q in range(8)]
    for table in tables:
        table.wait()
    for j in range(HALF_CLASSES):
        rows = slice(32 * j, 32 * j + 32)
        cos, sin = twist_ref[j, :, 0:256], twist_ref[j, :, 256:512]
        real = weighted([(small(j, q)[0], signal[q]) for q in range(8)])
        imag = weighted([(-small(j, q)[1], signal[q]) for q in range(8)])
        if imag is None:
            left[0, rows] = real * cos
            left[1, rows] = -real * sin
        else:
            left[0, rows] = real * cos + imag * sin
            left[1, rows] = imag * cos - real * sin
    transform()
    for j in range(HALF_CLASSES):
        rows = slice(32 * j, 32 * j + 32)
        h_real = h_ref[j // 2, 0, j % 2].astype(jnp.float32)
        h_imag = h_ref[j // 2, 1, j % 2].astype(jnp.float32)
        if 0 < j < 8:
            h_real = h_real + h_ref[(16 - j) // 2, 0, j % 2].astype(jnp.float32)
            h_imag = h_imag - h_ref[(16 - j) // 2, 1, j % 2].astype(jnp.float32)
        real = right[0, rows, 0:256] + right[1, rows, 256:512]
        imag = right[1, rows, 0:256] - right[0, rows, 256:512]
        left[0, rows] = real * h_real - imag * h_imag
        left[1, rows] = real * h_imag + imag * h_real
    transform()
    reals, imags = [], []
    for j in range(HALF_CLASSES):
        rows = slice(32 * j, 32 * j + 32)
        cos, sin = twist_ref[j, :, 0:256], twist_ref[j, :, 256:512]
        real = right[0, rows, 0:256] - right[1, rows, 256:512]
        imag = right[1, rows, 0:256] + right[0, rows, 256:512]
        reals.append(real * cos - imag * sin)
        imags.append(real * sin + imag * cos)
    skip = skip_ref[...]
    for q in range(8):
        terms = [(small(j, q)[0], reals[j]) for j in range(HALF_CLASSES)]
        terms += [(-small(j, q)[1], imags[j]) for j in range(HALF_CLASSES)]
        convolved = weighted(terms) * (1.0 / 4096)
        out_ref[q] = (gate[q] * (convolved + skip * drive[q])).astype(out_ref.dtype)


def filtered(where, pieces, spectrum, skip):
    high, low, twist = tables()
    vmem = pl.BlockSpec(memory_space=pltpu.VMEM)
    return pl.pallas_call(
        filter_kernel,
        out_shape=jax.ShapeDtypeStruct((8, 32, 256), jnp.bfloat16),
        in_specs=[pl.BlockSpec(memory_space=pltpu.SMEM)]
        + [vmem]
        + [pl.BlockSpec(memory_space=pl.ANY)] * 8,
        out_specs=vmem,
        scratch_shapes=[
            pltpu.VMEM((8, 32, 256), jnp.float32),
            pltpu.VMEM((8, 32, 256), jnp.float32),
            pltpu.VMEM((2, 32 * HALF_CLASSES, 256), jnp.float32),
            pltpu.VMEM((2, 32 * HALF_CLASSES, 512), jnp.float32),
            pltpu.VMEM((8, 2, 2, 32, 256), jnp.bfloat16),
            pltpu.VMEM((256, 512), jnp.bfloat16),
            pltpu.VMEM((256, 512), jnp.bfloat16),
            pltpu.VMEM((HALF_CLASSES, 1, 512), jnp.float32),
            pltpu.VMEM((4, 96, 512), jnp.float32),
            pltpu.SemaphoreType.DMA((8,)),
        ],
        compiler_params=pltpu.CompilerParams(vmem_limit_bytes=16 * 1024 * 1024),
        cost_estimate=cost(3),
    )(where, skip, *pieces, spectrum, high, low, twist)


def turned_filter(filter_spectrum):
    first = 2 * (NC * lax.axis_index("x") + lax.axis_index("core"))
    eye = np.eye(256, dtype=np.float32)
    own = first + jnp.arange(2, dtype=jnp.int32)
    order = jnp.where((own <= 8)[:, None, None], eye[None], eye[None, :, ::-1])
    turned = jnp.einsum(
        "plgc,lgh->plch",
        filter_spectrum.astype(jnp.bfloat16),
        order.astype(jnp.bfloat16),
        preferred_element_type=jnp.float32,
    ).astype(jnp.bfloat16)
    return turned.reshape(2, 2, 8, 32, 256).transpose(2, 0, 1, 3, 4)


def block_spots(core, z):
    side = jnp.where(z % 2 == 0, 3, 1)
    quarters = [z // 2, z // 2 + side, z // 2 + 4 - side, z // 2 + 2]
    return [2 * (quarter % 4) + core for quarter in quarters]


def cost(microseconds):
    return pl.CostEstimate(
        flops=int(microseconds * 1e9), bytes_accessed=int(microseconds * 3e6), transcendentals=0
    )


def turn_kernel(place_ref, own_ref, sibling_ref, hbm_ref, turned, out_ref, sems):
    z, y, core, x = (place_ref[i] for i in range(4))

    def turn(piece, feature, y_at):
        def put(ref):
            for part in range(3):
                turned[part] = ref[part, y_at].T

        pl.when(feature == core)(lambda: put(own_ref))
        pl.when(feature != core)(lambda: put(sibling_ref))
        columns = slice(256 * (piece % 4), 256 * (piece % 4) + 256)
        for k in range(4):
            for side in range(2):
                start = pl.multiple_of(32 * (2 * ((x + k) % 4) + (core + side) % 2), 32)
                for part in range(3):
                    row = 192 * k + 96 * side + 32 * part
                    out_ref[piece // 4, row : row + 32, columns] = turned[part, pl.ds(start, 32)]

    copies = []
    for half in range(2):
        for piece in range(4 * half, 4 * half + 4):
            turn(piece, (z + half) % 2, (y + piece) % 4)
        copies += copy_all([(out_ref.at[half], hbm_ref.at[half])], sems.at[pl.ds(half, 1)])
    for copy in copies:
        copy.wait()


def turned_weight(where, own, sibling):
    vmem = pl.BlockSpec(memory_space=pltpu.VMEM)
    return pl.pallas_call(
        turn_kernel,
        out_shape=jax.ShapeDtypeStruct((2, 768, 1024), jnp.bfloat16),
        in_specs=[pl.BlockSpec(memory_space=pltpu.SMEM), vmem, vmem],
        out_specs=pl.BlockSpec(memory_space=pltpu.HBM),
        scratch_shapes=[
            pltpu.VMEM((3, 256, 256), jnp.bfloat16),
            pltpu.VMEM((2, 768, 1024), jnp.bfloat16),
            pltpu.SemaphoreType.DMA((2,)),
        ],
        compiler_params=pltpu.CompilerParams(vmem_limit_bytes=16 * 1024 * 1024),
        cost_estimate=cost(3),
    )(where, own.reshape(3, 4, 256, 256), sibling.reshape(3, 4, 256, 256))


def copy_all(pairs, sems):
    copies = [
        pltpu.make_async_copy(source, target, sems.at[index])
        for index, (source, target) in enumerate(pairs)
    ]
    for copy in copies:
        copy.start()
    return copies


def join_kernel(*refs):
    parts, out_refs = refs[:4], refs[4:6]
    for k, part in enumerate(parts):
        for half, out_ref in enumerate(out_refs):
            out_ref[:, 256 * k : 256 * k + 256] = part[128 * half : 128 * half + 128]


def joined(parts):
    vmem = pl.BlockSpec(memory_space=pltpu.VMEM)
    return pl.pallas_call(
        join_kernel,
        out_shape=[jax.ShapeDtypeStruct((128, 1024), jnp.bfloat16)] * 2,
        in_specs=[vmem] * 4,
        out_specs=[vmem] * 2,
        cost_estimate=cost(2),
    )(*parts)


def slot_kernel(blocks, count, place_ref, *refs):
    sources, out_refs = refs[: 2 * count + 1], refs[2 * count + 1 : 2 * count + 5]
    unit_ref, weight_ref, sems = refs[2 * count + 5 :]
    pairs = [
        (sources[index], unit_ref.at[index // 2, pl.ds(128 * (index % 2), 128)])
        for index in range(2 * count)
    ]
    copies = copy_all(pairs + [(sources[-1], weight_ref)], sems)
    for copy in copies:
        copy.wait()

    def run(case):
        for index, block in enumerate(blocks):
            total = sum(
                lax.dot_general(
                    weight_ref[half], unit_ref[unit], (((1,), (1,)), ((), ())),
                    preferred_element_type=jnp.float32,
                )
                for unit, half in block[case]
            )
            columns = slice(256 * index, 256 * index + 256)
            for k, out_ref in enumerate(out_refs):
                rows = slice(192 * k, 192 * k + 192)
                out_ref[:, columns] = total[rows].astype(out_ref.dtype)

    for number in range(2):
        pl.when(place_ref[0] % 2 == number)(functools.partial(run, number))


def slot(where, units, weight, *blocks):
    names = sorted({name for block in blocks for case in block for name, _ in case})
    order = {name: index for index, name in enumerate(names)}
    blocks = [[[(order[name], half) for name, half in case] for case in block] for block in blocks]
    vmem = pl.BlockSpec(memory_space=pltpu.VMEM)
    anywhere = pl.BlockSpec(memory_space=pl.ANY)
    shape = (192, 256 * len(blocks))
    return pl.pallas_call(
        functools.partial(slot_kernel, blocks, len(names)),
        out_shape=[jax.ShapeDtypeStruct(shape, jnp.float32)]
        + [jax.ShapeDtypeStruct(shape, jnp.bfloat16)] * 3,
        in_specs=[pl.BlockSpec(memory_space=pltpu.SMEM)]
        + [anywhere] * (2 * len(names))
        + [pl.BlockSpec(memory_space=pltpu.HBM)],
        out_specs=[vmem] * 4,
        scratch_shapes=[
            pltpu.VMEM((len(names), 256, 1024), jnp.bfloat16),
            pltpu.VMEM((2, 768, 1024), jnp.bfloat16),
            pltpu.SemaphoreType.DMA((2 * len(names) + 1,)),
        ],
        compiler_params=pltpu.CompilerParams(vmem_limit_bytes=16 * 1024 * 1024),
        cost_estimate=cost(3),
    )(where, *[half for name in names for half in units[name]], weight)


def sum_over_x(parts):
    total = parts[0]
    for k in (1, 2, 3):
        total = total + shift(parts[k], "x", k).astype(jnp.float32)
    return total[:96], shift(total[96:], "core", 1)


def mix_kernel(place_ref, *refs):
    blocks, weights, out_ref, ordered = refs[:8], refs[8:10], refs[10], refs[11]
    z, y, core = place_ref[0], place_ref[1], place_ref[2]
    for k, step in enumerate((0, 1, 2, 7, 6, 3, 5, 4)):
        ordered[(z + step + 4 * core) % 8] = blocks[k][...]
    for column in range(4):
        total = sum(
            jnp.dot(
                ordered[4 * side + row], weights[side][column, row],
                preferred_element_type=jnp.float32,
            )
            for side in range(2)
            for row in range(4)
        )
        out_ref[(y + column) % 4] = total.astype(out_ref.dtype)


def mix(where, blocks, weights):
    vmem = pl.BlockSpec(memory_space=pltpu.VMEM)
    return pl.pallas_call(
        mix_kernel,
        out_shape=jax.ShapeDtypeStruct((4, 256, 256), jnp.bfloat16),
        in_specs=[pl.BlockSpec(memory_space=pltpu.SMEM)] + [vmem] * 10,
        out_specs=vmem,
        scratch_shapes=[pltpu.VMEM((8, 256, 256), jnp.bfloat16)],
        compiler_params=pltpu.CompilerParams(vmem_limit_bytes=16 * 1024 * 1024),
        cost_estimate=cost(2),
    )(where, *blocks, *weights)


def over_ctx(values):
    return lax.all_to_all(values, CTX, split_axis=0, concat_axis=0, tiled=True)


def shards(tokens, in_weight, filter_spectrum, skip_gain, out_weight):
    x, core = lax.axis_index("x"), lax.axis_index("core")
    z, y = lax.axis_index("z"), lax.axis_index("y")
    where = jnp.stack([z, y, core, x]).astype(jnp.int32)

    block = lax.ppermute(tokens, EVERY, MOVE)
    sibling = shift(in_weight, "core", 1)
    sent_filter = turned_filter(filter_spectrum)
    skip = lax.dynamic_slice_in_dim(skip_gain, 32 * (NC * x + core), 32)[:, None]
    spectrum = over_ctx(sent_filter)
    blocks = [block] + [shift(block, "y", -k) for k in (1, 2, 3)]

    out_weight, _ = together(out_weight, block)
    mine = lax.dynamic_index_in_dim(
        out_weight.reshape(2, 4, 4, 256, 256), core, 0, keepdims=False
    )
    rows = [
        lax.dynamic_index_in_dim(mine, (y + 4 - k) % 4, 1, keepdims=False) for k in range(4)
    ]
    halves = joined(blocks)
    spectrum, halves, rows = together(spectrum, halves, rows)
    units = {"own": halves}
    up, down = ([shift(half, "z", step) for half in halves] for step in (1, -1))
    units["up1"], units["down1"] = up, down
    rows[1] = shift(rows[1], "y", -1)

    weight = turned_weight(where, in_weight, sibling)
    weight, last = together(weight, [up[1], down[1]])
    up, down = (
        [shift(first, "z", step), shift(second, "z", step)]
        for first, second, step in ((up[0], last[0], 1), (down[0], last[1], -1))
    )
    units["up2"], units["down2"] = up, down

    rows[1], rows[3], last = together(rows[1], rows[3], [up[1], down[1]])
    rows[3] = shift(rows[3], "y", -3)
    up, down = (
        [shift(first, "z", step), shift(second, "z", step)]
        for first, second, step in ((up[0], last[0], 1), (down[0], last[1], -1))
    )
    units["up3"], units["down3"] = up, down
    parts = slot(
        where, units, weight,
        [[("own", 0), ("down1", 1)], [("own", 0), ("up1", 1)]],
        [[("up1", 1), ("up2", 0)], [("down1", 1), ("down2", 0)]],
    )
    parts, rows[3], last = together(parts, rows[3], down[1])
    pieces = [sum_over_x(parts)]

    units["across"] = [shift(up[0], "z", 1), shift(last, "z", -1)]
    pieces[0], units["across"] = together(pieces[0], units["across"])
    parts = slot(
        where, units, weight,
        [[("down2", 0), ("down3", 1)], [("up2", 0), ("up3", 1)]],
        [[("up3", 1), ("across", 0)], [("down3", 1), ("across", 0)]],
    )
    pieces.append(sum_over_x(parts))
    pieces = [piece[0] for piece in pieces] + [piece[1] for piece in pieces]

    gated = filtered(where, pieces, spectrum, skip)
    rows[2], _ = together(rows[2], gated)
    rows[2] = shift(rows[2], "y", -2)
    gated = over_ctx(gated).reshape(256, 256).T
    plus2, minus2, plus1, minus1 = near_z(gated)
    rows, _ = together(rows, plus1)
    rows = jnp.stack(rows)
    blocks = [gated, plus1, plus2, minus1, minus2] + far_z(plus2, minus2)
    partial = mix(where, blocks, [rows, shift(rows, "core", 1)])
    parts = lax.all_to_all(partial, "y", split_axis=0, concat_axis=0, tiled=True)
    return jnp.sum(parts.astype(jnp.float32), 0).astype(jnp.bfloat16)


def solution(mesh):
    fine = Mesh(mesh.devices.reshape(NX, NC, NZ, NY), EVERY)
    tp = ("z", "y")
    placed = (P(CTX, tp), P(None, CTX, tp), P(None, CTX, None, tp), P(tp), P(None, tp))
    return jax.shard_map(
        shards, mesh=fine, in_specs=placed, out_specs=P(CTX, tp), check_vma=False
    )
```

```python
import functools
import math

import jax
import jax.numpy as jnp
import ml_dtypes
import numpy as np
from jax import lax
from jax.experimental import pallas as pl
from jax.experimental.pallas import tpu as pltpu
from jax.sharding import Mesh, PartitionSpec as P

NX, NC, NZ, NY = 4, 2, 8, 4
SIZES = dict(x=NX, core=NC, z=NZ, y=NY)
EVERY = ("x", "core", "z", "y")
CTX = ("x", "core")
HALF_CLASSES = 9


def place(x, core, z, y):
    return ((x * NC + core) * NZ + z) * NY + y


MOVE = [
    (place(p, core, 2 * x + f, y), place(x, core, 2 * p + f, y))
    for p in range(4)
    for core in range(2)
    for x in range(4)
    for f in range(2)
    for y in range(4)
]


def shift(values, axis, step):
    n = SIZES[axis]
    return lax.ppermute(values, axis, [(i, (i + step) % n) for i in range(n)])


def near_and_far(block):
    half = block.shape[0] // 2
    plus1, minus1 = shift(block, "z", -1), shift(block, "z", 1)
    plus2, minus2 = shift(block, "z", -2), shift(block, "z", 2)
    plus1, minus1, plus2, minus2 = together(plus1, minus1, plus2, minus2)
    plus3, minus3 = shift(plus2, "z", -1), shift(minus2, "z", 1)
    plus4 = [shift(plus2[:half], "z", -2), shift(minus2[half:], "z", 2)]
    return [block, plus1, plus2, minus1, minus2, plus3, minus3, jnp.concatenate(plus4, 0)]


def together(*values):
    return lax.optimization_barrier(values)


@functools.lru_cache(None)
def tables():
    r = np.arange(256)
    big = 2 * np.pi * (np.outer(r, r) % 256) / 256
    c, s = np.cos(big), np.sin(big)
    both = np.concatenate([c, s], 1).astype(np.float32)
    high = both.astype(ml_dtypes.bfloat16)
    low = (both - high.astype(np.float32)).astype(ml_dtypes.bfloat16)
    j = np.arange(HALF_CLASSES)
    turn = 2 * np.pi * np.outer(j, r) / 4096
    twist = np.concatenate([np.cos(turn), np.sin(turn)], 1).astype(np.float32)
    return high, low, twist[:, None, :]


def small(j, q):
    turn = 2 * math.pi * ((j * q) % 16) / 16
    return round(math.cos(turn), 12), round(math.sin(turn), 12)


def weighted(terms):
    total = None
    for scale, value in terms:
        if scale == 0.0:
            continue
        part = value if scale == 1.0 else -value if scale == -1.0 else scale * value
        total = part if total is None else total + part
    return total


def filter_kernel(
    place_ref, *refs,
):
    (
        skip_ref, sources, out_ref,
        (drive, gate, left, right, h_ref, high_ref, low_ref, twist_ref, piece_ref, sems),
    ) = refs[0], refs[1:9], refs[9], refs[10:]
    targets = [piece_ref.at[k] for k in range(4)] + [h_ref, high_ref, low_ref, twist_ref]
    copies = copy_all(zip(sources, targets), sems)
    tables = copies[4:]
    for copy in copies[:4]:
        copy.wait()

    def transform():
        for part in range(2):
            values = left[part]
            high = values.astype(jnp.bfloat16)
            low = (values - high.astype(jnp.float32)).astype(jnp.bfloat16)
            right[part] = sum(
                jnp.dot(a, b[...], preferred_element_type=jnp.float32)
                for a, b in ((high, high_ref), (high, low_ref), (low, high_ref))
            )

    z, own = place_ref[0], place_ref[2]
    for side, core in enumerate((own, 1 - own)):
        spots = block_spots(core, z)
        for q, (index, column) in zip(spots, ((0, 0), (0, 256), (1, 0), (1, 256))):
            total = piece_ref[2 * side + index, :, column : column + 256]
            gate[q] = total[0:32]
            drive[q] = total[32:64] * total[64:96]
    signal = [drive[q] for q in range(8)]
    for table in tables:
        table.wait()
    for j in range(HALF_CLASSES):
        rows = slice(32 * j, 32 * j + 32)
        cos, sin = twist_ref[j, :, 0:256], twist_ref[j, :, 256:512]
        real = weighted([(small(j, q)[0], signal[q]) for q in range(8)])
        imag = weighted([(-small(j, q)[1], signal[q]) for q in range(8)])
        if imag is None:
            left[0, rows] = real * cos
            left[1, rows] = -real * sin
        else:
            left[0, rows] = real * cos + imag * sin
            left[1, rows] = imag * cos - real * sin
    transform()
    for j in range(HALF_CLASSES):
        rows = slice(32 * j, 32 * j + 32)
        h_real = h_ref[j // 2, 0, j % 2].astype(jnp.float32)
        h_imag = h_ref[j // 2, 1, j % 2].astype(jnp.float32)
        if 0 < j < 8:
            h_real = h_real + h_ref[(16 - j) // 2, 0, j % 2].astype(jnp.float32)
            h_imag = h_imag - h_ref[(16 - j) // 2, 1, j % 2].astype(jnp.float32)
        real = right[0, rows, 0:256] + right[1, rows, 256:512]
        imag = right[1, rows, 0:256] - right[0, rows, 256:512]
        left[0, rows] = real * h_real - imag * h_imag
        left[1, rows] = real * h_imag + imag * h_real
    transform()
    reals, imags = [], []
    for j in range(HALF_CLASSES):
        rows = slice(32 * j, 32 * j + 32)
        cos, sin = twist_ref[j, :, 0:256], twist_ref[j, :, 256:512]
        real = right[0, rows, 0:256] - right[1, rows, 256:512]
        imag = right[1, rows, 0:256] + right[0, rows, 256:512]
        reals.append(real * cos - imag * sin)
        imags.append(real * sin + imag * cos)
    skip = skip_ref[...]
    for q in range(8):
        terms = [(small(j, q)[0], reals[j]) for j in range(HALF_CLASSES)]
        terms += [(-small(j, q)[1], imags[j]) for j in range(HALF_CLASSES)]
        convolved = weighted(terms) * (1.0 / 4096)
        out_ref[q] = (gate[q] * (convolved + skip * drive[q])).astype(out_ref.dtype)


def filtered(where, pieces, spectrum, skip):
    high, low, twist = tables()
    vmem = pl.BlockSpec(memory_space=pltpu.VMEM)
    return pl.pallas_call(
        filter_kernel,
        out_shape=jax.ShapeDtypeStruct((8, 32, 256), jnp.bfloat16),
        in_specs=[pl.BlockSpec(memory_space=pltpu.SMEM)]
        + [vmem]
        + [pl.BlockSpec(memory_space=pl.ANY)] * 8,
        out_specs=vmem,
        scratch_shapes=[
            pltpu.VMEM((8, 32, 256), jnp.float32),
            pltpu.VMEM((8, 32, 256), jnp.float32),
            pltpu.VMEM((2, 32 * HALF_CLASSES, 256), jnp.float32),
            pltpu.VMEM((2, 32 * HALF_CLASSES, 512), jnp.float32),
            pltpu.VMEM((8, 2, 2, 32, 256), jnp.bfloat16),
            pltpu.VMEM((256, 512), jnp.bfloat16),
            pltpu.VMEM((256, 512), jnp.bfloat16),
            pltpu.VMEM((HALF_CLASSES, 1, 512), jnp.float32),
            pltpu.VMEM((4, 96, 512), jnp.float32),
            pltpu.SemaphoreType.DMA((8,)),
        ],
        compiler_params=pltpu.CompilerParams(vmem_limit_bytes=16 * 1024 * 1024),
        cost_estimate=cost(3),
    )(where, skip, *pieces, spectrum, high, low, twist)


def turned_filter(filter_spectrum):
    first = 2 * (NC * lax.axis_index("x") + lax.axis_index("core"))
    eye = np.eye(256, dtype=np.float32)
    own = first + jnp.arange(2, dtype=jnp.int32)
    order = jnp.where((own <= 8)[:, None, None], eye[None], eye[None, :, ::-1])
    turned = jnp.einsum(
        "plgc,lgh->plch",
        filter_spectrum.astype(jnp.bfloat16),
        order.astype(jnp.bfloat16),
        preferred_element_type=jnp.float32,
    ).astype(jnp.bfloat16)
    return turned.reshape(2, 2, 8, 32, 256).transpose(2, 0, 1, 3, 4)


def block_spots(core, z):
    side = jnp.where(z % 2 == 0, 3, 1)
    quarters = [z // 2, z // 2 + side, z // 2 + 4 - side, z // 2 + 2]
    return [2 * (quarter % 4) + core for quarter in quarters]


def cost(microseconds):
    return pl.CostEstimate(
        flops=int(microseconds * 1e9), bytes_accessed=int(microseconds * 3e6), transcendentals=0
    )


def turn_kernel(place_ref, own_ref, sibling_ref, hbm_ref, turned, out_ref, sems):
    z, y, core, x = (place_ref[i] for i in range(4))

    def turn(piece, carry):
        half, k = piece // 4, piece % 4
        own = (z + half) % 2 == core

        def put(ref):
            for part in range(3):
                turned[part] = ref[part, (y + k) % 4].T

        pl.when(own)(lambda: put(own_ref))
        pl.when(jnp.logical_not(own))(lambda: put(sibling_ref))
        columns = pl.ds(pl.multiple_of(256 * k, 256), 256)
        for k_out in range(4):
            for side in range(2):
                start = pl.multiple_of(32 * (2 * ((x + k_out) % 4) + (core + side) % 2), 32)
                for part in range(3):
                    row = 192 * k_out + 96 * side + 32 * part
                    out_ref[half, row : row + 32, columns] = turned[part, pl.ds(start, 32)]
        return carry

    lax.fori_loop(0, 8, turn, 0)
    copies = copy_all([(out_ref.at[half], hbm_ref.at[half]) for half in range(2)], sems)
    for copy in copies:
        copy.wait()


def turned_weight(where, own, sibling):
    vmem = pl.BlockSpec(memory_space=pltpu.VMEM)
    return pl.pallas_call(
        turn_kernel,
        out_shape=jax.ShapeDtypeStruct((2, 768, 1024), jnp.bfloat16),
        in_specs=[pl.BlockSpec(memory_space=pltpu.SMEM), vmem, vmem],
        out_specs=pl.BlockSpec(memory_space=pltpu.HBM),
        scratch_shapes=[
            pltpu.VMEM((3, 256, 256), jnp.bfloat16),
            pltpu.VMEM((2, 768, 1024), jnp.bfloat16),
            pltpu.SemaphoreType.DMA((2,)),
        ],
        compiler_params=pltpu.CompilerParams(vmem_limit_bytes=16 * 1024 * 1024),
        cost_estimate=cost(3),
    )(where, own.reshape(3, 4, 256, 256), sibling.reshape(3, 4, 256, 256))


def copy_all(pairs, sems):
    copies = [
        pltpu.make_async_copy(source, target, sems.at[index])
        for index, (source, target) in enumerate(pairs)
    ]
    for copy in copies:
        copy.start()
    return copies


def join_kernel(*refs):
    parts, out_refs = refs[:4], refs[4:6]
    for k, part in enumerate(parts):
        for half, out_ref in enumerate(out_refs):
            out_ref[:, 256 * k : 256 * k + 256] = part[128 * half : 128 * half + 128]


def joined(parts):
    vmem = pl.BlockSpec(memory_space=pltpu.VMEM)
    return pl.pallas_call(
        join_kernel,
        out_shape=[jax.ShapeDtypeStruct((128, 1024), jnp.bfloat16)] * 2,
        in_specs=[vmem] * 4,
        out_specs=[vmem] * 2,
        cost_estimate=cost(2),
    )(*parts)


def slot_kernel(blocks, count, place_ref, *refs):
    sources, out_refs = refs[: 2 * count + 1], refs[2 * count + 1 : 2 * count + 5]
    unit_ref, weight_ref, sems = refs[2 * count + 5 :]
    pairs = [
        (sources[index], unit_ref.at[index // 2, pl.ds(128 * (index % 2), 128)])
        for index in range(2 * count)
    ]
    copies = copy_all(pairs + [(sources[-1], weight_ref)], sems)
    for copy in copies:
        copy.wait()

    odd = place_ref[0] % 2

    def run(index, carry):
        total = 0.0
        for half in range(2):
            unit = 0
            for number, block in enumerate(blocks):
                even_unit, odd_unit = (
                    [name for name, side in case if side == half][0] for case in block
                )
                unit = jnp.where(index == number, jnp.where(odd, odd_unit, even_unit), unit)
            total += lax.dot_general(
                weight_ref[half], unit_ref[unit], (((1,), (1,)), ((), ())),
                preferred_element_type=jnp.float32,
            )
        columns = pl.ds(pl.multiple_of(256 * index, 256), 256)
        for k, out_ref in enumerate(out_refs):
            rows = slice(192 * k, 192 * k + 192)
            out_ref[:, columns] = total[rows].astype(out_ref.dtype)
        return carry

    lax.fori_loop(0, len(blocks), run, 0)


def slot(where, units, weight, *blocks):
    names = sorted({name for block in blocks for case in block for name, _ in case})
    order = {name: index for index, name in enumerate(names)}
    blocks = [[[(order[name], half) for name, half in case] for case in block] for block in blocks]
    vmem = pl.BlockSpec(memory_space=pltpu.VMEM)
    anywhere = pl.BlockSpec(memory_space=pl.ANY)
    shape = (192, 256 * len(blocks))
    return pl.pallas_call(
        functools.partial(slot_kernel, blocks, len(names)),
        out_shape=[jax.ShapeDtypeStruct(shape, jnp.float32)]
        + [jax.ShapeDtypeStruct(shape, jnp.bfloat16)] * 3,
        in_specs=[pl.BlockSpec(memory_space=pltpu.SMEM)]
        + [anywhere] * (2 * len(names))
        + [pl.BlockSpec(memory_space=pltpu.HBM)],
        out_specs=[vmem] * 4,
        scratch_shapes=[
            pltpu.VMEM((len(names), 256, 1024), jnp.bfloat16),
            pltpu.VMEM((2, 768, 1024), jnp.bfloat16),
            pltpu.SemaphoreType.DMA((2 * len(names) + 1,)),
        ],
        compiler_params=pltpu.CompilerParams(vmem_limit_bytes=16 * 1024 * 1024),
        cost_estimate=cost(3),
    )(where, *[half for name in names for half in units[name]], weight)


def sum_over_x(parts):
    total = parts[0]
    for k in (1, 2, 3):
        total = total + shift(parts[k], "x", k).astype(jnp.float32)
    return total[:96], shift(total[96:], "core", 1)


def mix_kernel(place_ref, *refs):
    blocks, weights, out_ref, ordered = refs[:8], refs[8:10], refs[10], refs[11]
    z, core = place_ref[0], place_ref[2]
    for k, step in enumerate((0, 1, 2, 7, 6, 3, 5, 4)):
        ordered[(z + step + 4 * core) % 8] = blocks[k][...]

    def mix_column(column, carry):
        total = sum(
            jnp.dot(
                ordered[4 * side + row], weights[side][column, row],
                preferred_element_type=jnp.float32,
            )
            for side in range(2)
            for row in range(4)
        )
        out_ref[column] = total.astype(out_ref.dtype)
        return carry

    lax.fori_loop(0, 4, mix_column, 0)


def mix(where, blocks, weights):
    vmem = pl.BlockSpec(memory_space=pltpu.VMEM)
    return pl.pallas_call(
        mix_kernel,
        out_shape=jax.ShapeDtypeStruct((4, 256, 256), jnp.bfloat16),
        in_specs=[pl.BlockSpec(memory_space=pltpu.SMEM)] + [vmem] * 10,
        out_specs=vmem,
        scratch_shapes=[pltpu.VMEM((8, 256, 256), jnp.bfloat16)],
        compiler_params=pltpu.CompilerParams(vmem_limit_bytes=16 * 1024 * 1024),
        cost_estimate=cost(2),
    )(where, *blocks, *weights)


def over_ctx(values):
    return lax.all_to_all(values, CTX, split_axis=0, concat_axis=0, tiled=True)


def shards(tokens, in_weight, filter_spectrum, skip_gain, out_weight):
    x, core = lax.axis_index("x"), lax.axis_index("core")
    z, y = lax.axis_index("z"), lax.axis_index("y")
    where = jnp.stack([z, y, core, x]).astype(jnp.int32)

    block = lax.ppermute(tokens, EVERY, MOVE)
    sibling = shift(in_weight, "core", 1)
    sent_filter = turned_filter(filter_spectrum)
    skip = lax.dynamic_slice_in_dim(skip_gain, 32 * (NC * x + core), 32)[:, None]
    spectrum = over_ctx(sent_filter)
    blocks = [block] + [shift(block, "y", -k) for k in (1, 2, 3)]

    out_weight, _ = together(out_weight, block)
    mine = lax.dynamic_index_in_dim(
        out_weight.reshape(2, 4, 4, 256, 256), core, 0, keepdims=False
    )
    rows = [
        lax.dynamic_index_in_dim(mine, (y + 4 - k) % 4, 1, keepdims=False) for k in range(4)
    ]
    halves = joined(blocks)
    spectrum, halves, rows = together(spectrum, halves, rows)
    units = {"own": halves}
    up, down = ([shift(half, "z", step) for half in halves] for step in (1, -1))
    units["up1"], units["down1"] = up, down
    rows[1] = shift(rows[1], "y", -1)

    weight = turned_weight(where, in_weight, sibling)
    weight, last = together(weight, [up[1], down[1]])
    up, down = (
        [shift(first, "z", step), shift(second, "z", step)]
        for first, second, step in ((up[0], last[0], 1), (down[0], last[1], -1))
    )
    units["up2"], units["down2"] = up, down

    rows[1], rows[3], last = together(rows[1], rows[3], [up[1], down[1]])
    rows[3] = shift(rows[3], "y", -3)
    up, down = (
        [shift(first, "z", step), shift(second, "z", step)]
        for first, second, step in ((up[0], last[0], 1), (down[0], last[1], -1))
    )
    units["up3"], units["down3"] = up, down
    parts = slot(
        where, units, weight,
        [[("own", 0), ("down1", 1)], [("own", 0), ("up1", 1)]],
        [[("up1", 1), ("up2", 0)], [("down1", 1), ("down2", 0)]],
    )
    parts, rows[3], last = together(parts, rows[3], down[1])
    pieces = [sum_over_x(parts)]

    units["across"] = [shift(up[0], "z", 1), shift(last, "z", -1)]
    pieces[0], units["across"] = together(pieces[0], units["across"])
    parts = slot(
        where, units, weight,
        [[("down2", 0), ("down3", 1)], [("up2", 0), ("up3", 1)]],
        [[("up3", 1), ("across", 0)], [("down3", 1), ("across", 0)]],
    )
    rows[2], _ = together(rows[2], parts[0])
    rows[2] = shift(rows[2], "y", -2)
    pieces.append(sum_over_x(parts))
    pieces = [piece[0] for piece in pieces] + [piece[1] for piece in pieces]

    gated = filtered(where, pieces, spectrum, skip)
    gated = over_ctx(gated).reshape(256, 256).T
    rows, _ = together(rows, gated)
    rows = jnp.stack(rows)
    partial = mix(where, near_and_far(gated), [rows, shift(rows, "core", 1)])
    total = partial[0].astype(jnp.float32)
    for k in (1, 2, 3):
        total = total + shift(partial[k], "y", k).astype(jnp.float32)
    return total.astype(jnp.bfloat16)


def solution(mesh):
    fine = Mesh(mesh.devices.reshape(NX, NC, NZ, NY), EVERY)
    tp = ("z", "y")
    placed = (P(CTX, tp), P(None, CTX, tp), P(None, CTX, None, tp), P(tp), P(None, tp))
    return jax.shard_map(
        shards, mesh=fine, in_specs=placed, out_specs=P(CTX, tp), check_vma=False
    )
```

```python
import functools
import math

import jax
import jax.numpy as jnp
import ml_dtypes
import numpy as np
from jax import lax
from jax.experimental import pallas as pl
from jax.experimental.pallas import tpu as pltpu
from jax.sharding import Mesh, PartitionSpec as P

NX, NC, NZ, NY = 4, 2, 8, 4
SIZES = dict(x=NX, core=NC, z=NZ, y=NY)
EVERY = ("x", "core", "z", "y")
CTX = ("x", "core")
HALF_CLASSES = 9


def place(x, core, z, y):
    return ((x * NC + core) * NZ + z) * NY + y


MOVE = [
    (place(p, core, 2 * x + f, y), place(x, core, 2 * p + f, y))
    for p in range(4)
    for core in range(2)
    for x in range(4)
    for f in range(2)
    for y in range(4)
]


def shift(values, axis, step):
    n = SIZES[axis]
    return lax.ppermute(values, axis, [(i, (i + step) % n) for i in range(n)])


def near_and_far(block):
    half = block.shape[0] // 2
    plus1, minus1 = shift(block, "z", -1), shift(block, "z", 1)
    plus2, minus2 = shift(block, "z", -2), shift(block, "z", 2)
    plus1, minus1, plus2, minus2 = together(plus1, minus1, plus2, minus2)
    plus3, minus3 = shift(plus2, "z", -1), shift(minus2, "z", 1)
    plus4 = [shift(plus2[:half], "z", -2), shift(minus2[half:], "z", 2)]
    return [block, plus1, plus2, minus1, minus2, plus3, minus3, jnp.concatenate(plus4, 0)]


def together(*values):
    return lax.optimization_barrier(values)


@functools.lru_cache(None)
def tables():
    r = np.arange(256)
    big = 2 * np.pi * (np.outer(r, r) % 256) / 256
    c, s = np.cos(big), np.sin(big)
    both = np.concatenate([c, s], 1).astype(np.float32)
    high = both.astype(ml_dtypes.bfloat16)
    low = (both - high.astype(np.float32)).astype(ml_dtypes.bfloat16)
    j = np.arange(HALF_CLASSES)
    turn = 2 * np.pi * np.outer(j, r) / 4096
    twist = np.concatenate([np.cos(turn), np.sin(turn)], 1).astype(np.float32)
    return high, low, twist[:, None, :]


def small(j, q):
    turn = 2 * math.pi * ((j * q) % 16) / 16
    return round(math.cos(turn), 12), round(math.sin(turn), 12)


def weighted(terms):
    total = None
    for scale, value in terms:
        if scale == 0.0:
            continue
        part = value if scale == 1.0 else -value if scale == -1.0 else scale * value
        total = part if total is None else total + part
    return total


def filter_kernel(
    place_ref, *refs,
):
    (
        skip_ref, sources, out_ref,
        (drive, gate, left, right, h_ref, high_ref, low_ref, twist_ref, piece_ref, sems),
    ) = refs[0], refs[1:9], refs[9], refs[10:]
    targets = [piece_ref.at[k] for k in range(4)] + [h_ref, high_ref, low_ref, twist_ref]
    copies = copy_all(zip(sources, targets), sems)
    tables = copies[4:]
    for copy in copies[:4]:
        copy.wait()

    def transform():
        for part in range(2):
            values = left[part]
            high = values.astype(jnp.bfloat16)
            low = (values - high.astype(jnp.float32)).astype(jnp.bfloat16)
            right[part] = sum(
                jnp.dot(a, b[...], preferred_element_type=jnp.float32)
                for a, b in ((high, high_ref), (high, low_ref), (low, high_ref))
            )

    z, own = place_ref[0], place_ref[2]
    for side, core in enumerate((own, 1 - own)):
        spots = block_spots(core, z)
        for q, (index, column) in zip(spots, ((0, 0), (0, 256), (1, 0), (1, 256))):
            total = piece_ref[2 * side + index, :, column : column + 256]
            gate[q] = total[0:32]
            drive[q] = total[32:64] * total[64:96]
    signal = [drive[q] for q in range(8)]
    for table in tables:
        table.wait()
    for j in range(HALF_CLASSES):
        rows = slice(32 * j, 32 * j + 32)
        cos, sin = twist_ref[j, :, 0:256], twist_ref[j, :, 256:512]
        real = weighted([(small(j, q)[0], signal[q]) for q in range(8)])
        imag = weighted([(-small(j, q)[1], signal[q]) for q in range(8)])
        if imag is None:
            left[0, rows] = real * cos
            left[1, rows] = -real * sin
        else:
            left[0, rows] = real * cos + imag * sin
            left[1, rows] = imag * cos - real * sin
    transform()
    for j in range(HALF_CLASSES):
        rows = slice(32 * j, 32 * j + 32)
        h_real = h_ref[j // 2, 0, j % 2].astype(jnp.float32)
        h_imag = h_ref[j // 2, 1, j % 2].astype(jnp.float32)
        if 0 < j < 8:
            h_real = h_real + h_ref[(16 - j) // 2, 0, j % 2].astype(jnp.float32)
            h_imag = h_imag - h_ref[(16 - j) // 2, 1, j % 2].astype(jnp.float32)
        real = right[0, rows, 0:256] + right[1, rows, 256:512]
        imag = right[1, rows, 0:256] - right[0, rows, 256:512]
        left[0, rows] = real * h_real - imag * h_imag
        left[1, rows] = real * h_imag + imag * h_real
    transform()
    reals, imags = [], []
    for j in range(HALF_CLASSES):
        rows = slice(32 * j, 32 * j + 32)
        cos, sin = twist_ref[j, :, 0:256], twist_ref[j, :, 256:512]
        real = right[0, rows, 0:256] - right[1, rows, 256:512]
        imag = right[1, rows, 0:256] + right[0, rows, 256:512]
        reals.append(real * cos - imag * sin)
        imags.append(real * sin + imag * cos)
    skip = skip_ref[...]
    for q in range(8):
        terms = [(small(j, q)[0], reals[j]) for j in range(HALF_CLASSES)]
        terms += [(-small(j, q)[1], imags[j]) for j in range(HALF_CLASSES)]
        convolved = weighted(terms) * (1.0 / 4096)
        out_ref[q] = (gate[q] * (convolved + skip * drive[q])).astype(out_ref.dtype)


def filtered(where, pieces, spectrum, skip):
    high, low, twist = tables()
    vmem = pl.BlockSpec(memory_space=pltpu.VMEM)
    return pl.pallas_call(
        filter_kernel,
        out_shape=jax.ShapeDtypeStruct((8, 32, 256), jnp.bfloat16),
        in_specs=[pl.BlockSpec(memory_space=pltpu.SMEM)]
        + [vmem]
        + [pl.BlockSpec(memory_space=pl.ANY)] * 8,
        out_specs=vmem,
        scratch_shapes=[
            pltpu.VMEM((8, 32, 256), jnp.float32),
            pltpu.VMEM((8, 32, 256), jnp.float32),
            pltpu.VMEM((2, 32 * HALF_CLASSES, 256), jnp.float32),
            pltpu.VMEM((2, 32 * HALF_CLASSES, 512), jnp.float32),
            pltpu.VMEM((8, 2, 2, 32, 256), jnp.bfloat16),
            pltpu.VMEM((256, 512), jnp.bfloat16),
            pltpu.VMEM((256, 512), jnp.bfloat16),
            pltpu.VMEM((HALF_CLASSES, 1, 512), jnp.float32),
            pltpu.VMEM((4, 96, 512), jnp.float32),
            pltpu.SemaphoreType.DMA((8,)),
        ],
        compiler_params=pltpu.CompilerParams(vmem_limit_bytes=16 * 1024 * 1024),
        cost_estimate=cost(3),
    )(where, skip, *pieces, spectrum, high, low, twist)


def turned_filter(filter_spectrum):
    first = 2 * (NC * lax.axis_index("x") + lax.axis_index("core"))
    eye = np.eye(256, dtype=np.float32)
    own = first + jnp.arange(2, dtype=jnp.int32)
    order = jnp.where((own <= 8)[:, None, None], eye[None], eye[None, :, ::-1])
    turned = jnp.einsum(
        "plgc,lgh->plch",
        filter_spectrum.astype(jnp.bfloat16),
        order.astype(jnp.bfloat16),
        preferred_element_type=jnp.float32,
    ).astype(jnp.bfloat16)
    return turned.reshape(2, 2, 8, 32, 256).transpose(2, 0, 1, 3, 4)


def block_spots(core, z):
    side = jnp.where(z % 2 == 0, 3, 1)
    quarters = [z // 2, z // 2 + side, z // 2 + 4 - side, z // 2 + 2]
    return [2 * (quarter % 4) + core for quarter in quarters]


def cost(microseconds):
    return pl.CostEstimate(
        flops=int(microseconds * 1e9), bytes_accessed=int(microseconds * 3e6), transcendentals=0
    )


def turn_kernel(place_ref, own_ref, sibling_ref, hbm_ref, turned, out_ref, sems):
    z, y, core, x = (place_ref[i] for i in range(4))

    def turn(piece, carry):
        half, k = piece // 4, piece % 4
        own = (z + half) % 2 == core

        def put(ref):
            for part in range(3):
                turned[part] = ref[part, (y + k) % 4].T

        pl.when(own)(lambda: put(own_ref))
        pl.when(jnp.logical_not(own))(lambda: put(sibling_ref))
        columns = pl.ds(pl.multiple_of(256 * k, 256), 256)
        for k_out in range(4):
            for side in range(2):
                start = pl.multiple_of(32 * (2 * ((x + k_out) % 4) + (core + side) % 2), 32)
                for part in range(3):
                    row = 192 * k_out + 96 * side + 32 * part
                    out_ref[half, row : row + 32, columns] = turned[part, pl.ds(start, 32)]
        return carry

    lax.fori_loop(0, 8, turn, 0)
    copies = copy_all([(out_ref.at[half], hbm_ref.at[half]) for half in range(2)], sems)
    for copy in copies:
        copy.wait()


def turned_weight(where, own, sibling):
    vmem = pl.BlockSpec(memory_space=pltpu.VMEM)
    return pl.pallas_call(
        turn_kernel,
        out_shape=jax.ShapeDtypeStruct((2, 768, 1024), jnp.bfloat16),
        in_specs=[pl.BlockSpec(memory_space=pltpu.SMEM), vmem, vmem],
        out_specs=pl.BlockSpec(memory_space=pltpu.HBM),
        scratch_shapes=[
            pltpu.VMEM((3, 256, 256), jnp.bfloat16),
            pltpu.VMEM((2, 768, 1024), jnp.bfloat16),
            pltpu.SemaphoreType.DMA((2,)),
        ],
        compiler_params=pltpu.CompilerParams(vmem_limit_bytes=16 * 1024 * 1024),
        cost_estimate=cost(3),
    )(where, own.reshape(3, 4, 256, 256), sibling.reshape(3, 4, 256, 256))


def copy_all(pairs, sems):
    copies = [
        pltpu.make_async_copy(source, target, sems.at[index])
        for index, (source, target) in enumerate(pairs)
    ]
    for copy in copies:
        copy.start()
    return copies


def join_kernel(*refs):
    parts, out_refs = refs[:4], refs[4:6]
    for k, part in enumerate(parts):
        for half, out_ref in enumerate(out_refs):
            out_ref[:, 256 * k : 256 * k + 256] = part[128 * half : 128 * half + 128]


def joined(parts):
    vmem = pl.BlockSpec(memory_space=pltpu.VMEM)
    return pl.pallas_call(
        join_kernel,
        out_shape=[jax.ShapeDtypeStruct((128, 1024), jnp.bfloat16)] * 2,
        in_specs=[vmem] * 4,
        out_specs=[vmem] * 2,
        cost_estimate=cost(2),
    )(*parts)


def slot_kernel(blocks, count, place_ref, *refs):
    sources, out_refs = refs[: 2 * count + 1], refs[2 * count + 1 : 2 * count + 5]
    unit_ref, weight_ref, sems = refs[2 * count + 5 :]
    pairs = [
        (sources[index], unit_ref.at[index // 2, pl.ds(128 * (index % 2), 128)])
        for index in range(2 * count)
    ]
    copies = copy_all(pairs + [(sources[-1], weight_ref)], sems)
    for copy in copies:
        copy.wait()

    odd = place_ref[0] % 2

    def run(index, carry):
        total = 0.0
        for half in range(2):
            unit = 0
            for number, block in enumerate(blocks):
                even_unit, odd_unit = (
                    [name for name, side in case if side == half][0] for case in block
                )
                unit = jnp.where(index == number, jnp.where(odd, odd_unit, even_unit), unit)
            total += lax.dot_general(
                weight_ref[half], unit_ref[unit], (((1,), (1,)), ((), ())),
                preferred_element_type=jnp.float32,
            )
        columns = pl.ds(pl.multiple_of(256 * index, 256), 256)
        for k, out_ref in enumerate(out_refs):
            rows = slice(192 * k, 192 * k + 192)
            out_ref[:, columns] = total[rows].astype(out_ref.dtype)
        return carry

    lax.fori_loop(0, len(blocks), run, 0)


def slot(where, units, weight, *blocks):
    names = sorted({name for block in blocks for case in block for name, _ in case})
    order = {name: index for index, name in enumerate(names)}
    blocks = [[[(order[name], half) for name, half in case] for case in block] for block in blocks]
    vmem = pl.BlockSpec(memory_space=pltpu.VMEM)
    anywhere = pl.BlockSpec(memory_space=pl.ANY)
    shape = (192, 256 * len(blocks))
    return pl.pallas_call(
        functools.partial(slot_kernel, blocks, len(names)),
        out_shape=[jax.ShapeDtypeStruct(shape, jnp.float32)]
        + [jax.ShapeDtypeStruct(shape, jnp.bfloat16)] * 3,
        in_specs=[pl.BlockSpec(memory_space=pltpu.SMEM)]
        + [anywhere] * (2 * len(names))
        + [pl.BlockSpec(memory_space=pltpu.HBM)],
        out_specs=[vmem] * 4,
        scratch_shapes=[
            pltpu.VMEM((len(names), 256, 1024), jnp.bfloat16),
            pltpu.VMEM((2, 768, 1024), jnp.bfloat16),
            pltpu.SemaphoreType.DMA((2 * len(names) + 1,)),
        ],
        compiler_params=pltpu.CompilerParams(vmem_limit_bytes=16 * 1024 * 1024),
        cost_estimate=cost(3),
    )(where, *[half for name in names for half in units[name]], weight)


def moved_over_x(parts):
    return [shift(parts[k], "x", k) for k in (1, 2, 3)]


def sum_over_x(own, moved):
    total = own
    for part in moved:
        total = total + part.astype(jnp.float32)
    return total[:96], shift(total[96:], "core", 1)


def mix_kernel(place_ref, *refs):
    blocks, weights, out_ref, ordered = refs[:8], refs[8:10], refs[10], refs[11]
    z, core = place_ref[0], place_ref[2]
    for k, step in enumerate((0, 1, 2, 7, 6, 3, 5, 4)):
        ordered[(z + step + 4 * core) % 8] = blocks[k][...]

    def mix_column(column, carry):
        total = sum(
            jnp.dot(
                ordered[4 * side + row], weights[side][column, row],
                preferred_element_type=jnp.float32,
            )
            for side in range(2)
            for row in range(4)
        )
        out_ref[column] = total.astype(out_ref.dtype)
        return carry

    lax.fori_loop(0, 4, mix_column, 0)


def mix(where, blocks, weights):
    vmem = pl.BlockSpec(memory_space=pltpu.VMEM)
    return pl.pallas_call(
        mix_kernel,
        out_shape=jax.ShapeDtypeStruct((4, 256, 256), jnp.bfloat16),
        in_specs=[pl.BlockSpec(memory_space=pltpu.SMEM)] + [vmem] * 10,
        out_specs=vmem,
        scratch_shapes=[pltpu.VMEM((8, 256, 256), jnp.bfloat16)],
        compiler_params=pltpu.CompilerParams(vmem_limit_bytes=16 * 1024 * 1024),
        cost_estimate=cost(2),
    )(where, *blocks, *weights)


def over_ctx(values):
    return lax.all_to_all(values, CTX, split_axis=0, concat_axis=0, tiled=True)


def shards(tokens, in_weight, filter_spectrum, skip_gain, out_weight):
    x, core = lax.axis_index("x"), lax.axis_index("core")
    z, y = lax.axis_index("z"), lax.axis_index("y")
    where = jnp.stack([z, y, core, x]).astype(jnp.int32)

    block = lax.ppermute(tokens, EVERY, MOVE)
    sibling = shift(in_weight, "core", 1)
    sent_filter = turned_filter(filter_spectrum)
    skip = lax.dynamic_slice_in_dim(skip_gain, 32 * (NC * x + core), 32)[:, None]
    spectrum = over_ctx(sent_filter)
    blocks = [block] + [shift(block, "y", -k) for k in (1, 2, 3)]

    out_weight, _ = together(out_weight, block)
    mine = lax.dynamic_index_in_dim(
        out_weight.reshape(2, 4, 4, 256, 256), core, 0, keepdims=False
    )
    rows = [
        lax.dynamic_index_in_dim(mine, (y + 4 - k) % 4, 1, keepdims=False) for k in range(4)
    ]
    halves = joined(blocks)
    spectrum, halves, rows = together(spectrum, halves, rows)
    units = {"own": halves}
    up, down = ([shift(half, "z", step) for half in halves] for step in (1, -1))
    units["up1"], units["down1"] = up, down
    rows[1] = shift(rows[1], "y", -1)

    weight = turned_weight(where, in_weight, sibling)
    weight, last = together(weight, [up[1], down[1]])
    up, down = (
        [shift(first, "z", step), shift(second, "z", step)]
        for first, second, step in ((up[0], last[0], 1), (down[0], last[1], -1))
    )
    units["up2"], units["down2"] = up, down

    rows[1], rows[3], last = together(rows[1], rows[3], [up[1], down[1]])
    rows[3] = shift(rows[3], "y", -3)
    up, down = (
        [shift(first, "z", step), shift(second, "z", step)]
        for first, second, step in ((up[0], last[0], 1), (down[0], last[1], -1))
    )
    units["up3"], units["down3"] = up, down
    parts = slot(
        where, units, weight,
        [[("own", 0), ("down1", 1)], [("own", 0), ("up1", 1)]],
        [[("up1", 1), ("up2", 0)], [("down1", 1), ("down2", 0)]],
    )
    parts, rows[3], last = together(parts, rows[3], down[1])
    early, _ = together(parts, [up[1], down[0]])
    moved = moved_over_x(early)

    units["across"] = [shift(up[0], "z", 1), shift(last, "z", -1)]
    parts = slot(
        where, units, weight,
        [[("down2", 0), ("down3", 1)], [("up2", 0), ("up3", 1)]],
        [[("up3", 1), ("across", 0)], [("down3", 1), ("across", 0)]],
    )
    rows[2], _ = together(rows[2], parts[0])
    rows[2] = shift(rows[2], "y", -2)
    parts, moved = together(parts, moved)
    pieces = [sum_over_x(early[0], moved), sum_over_x(parts[0], moved_over_x(parts))]
    pieces = [piece[0] for piece in pieces] + [piece[1] for piece in pieces]

    gated = filtered(where, pieces, spectrum, skip)
    gated = over_ctx(gated).reshape(256, 256).T
    rows, _ = together(rows, gated)
    rows = jnp.stack(rows)
    partial = mix(where, near_and_far(gated), [rows, shift(rows, "core", 1)])
    total = partial[0].astype(jnp.float32)
    for k in (1, 2, 3):
        total = total + shift(partial[k], "y", k).astype(jnp.float32)
    return total.astype(jnp.bfloat16)


def solution(mesh):
    fine = Mesh(mesh.devices.reshape(NX, NC, NZ, NY), EVERY)
    tp = ("z", "y")
    placed = (P(CTX, tp), P(None, CTX, tp), P(None, CTX, None, tp), P(tp), P(None, tp))
    return jax.shard_map(
        shards, mesh=fine, in_specs=placed, out_specs=P(CTX, tp), check_vma=False
    )
```

```python
import functools
import math

import jax
import jax.numpy as jnp
import ml_dtypes
import numpy as np
from jax import lax
from jax.experimental import pallas as pl
from jax.experimental.pallas import tpu as pltpu
from jax.sharding import Mesh, PartitionSpec as P

NX, NC, NZ, NY = 4, 2, 8, 4
SIZES = dict(x=NX, core=NC, z=NZ, y=NY)
EVERY = ("x", "core", "z", "y")
CTX = ("x", "core")
HALF_CLASSES = 9


def place(x, core, z, y):
    return ((x * NC + core) * NZ + z) * NY + y


MOVE = [
    (place(p, core, 2 * x + f, y), place(x, core, 2 * p + f, y))
    for p in range(4)
    for core in range(2)
    for x in range(4)
    for f in range(2)
    for y in range(4)
]


def shift(values, axis, step):
    n = SIZES[axis]
    return lax.ppermute(values, axis, [(i, (i + step) % n) for i in range(n)])


def near_and_far(block):
    half = block.shape[0] // 2
    plus1, minus1 = shift(block, "z", -1), shift(block, "z", 1)
    plus2, minus2 = shift(block, "z", -2), shift(block, "z", 2)
    plus1, minus1, plus2, minus2 = together(plus1, minus1, plus2, minus2)
    plus3, minus3 = shift(plus2, "z", -1), shift(minus2, "z", 1)
    plus4 = [shift(plus2[:half], "z", -2), shift(minus2[half:], "z", 2)]
    return [block, plus1, plus2, minus1, minus2, plus3, minus3, jnp.concatenate(plus4, 0)]


def together(*values):
    return lax.optimization_barrier(values)


@functools.lru_cache(None)
def tables():
    r = np.arange(256)
    big = 2 * np.pi * (np.outer(r, r) % 256) / 256
    c, s = np.cos(big), np.sin(big)
    both = np.concatenate([c, s], 1).astype(np.float32)
    high = both.astype(ml_dtypes.bfloat16)
    low = (both - high.astype(np.float32)).astype(ml_dtypes.bfloat16)
    j = np.arange(HALF_CLASSES)
    turn = 2 * np.pi * np.outer(j, r) / 4096
    twist = np.concatenate([np.cos(turn), np.sin(turn)], 1).astype(np.float32)
    return high, low, twist[:, None, :]


def small(j, q):
    turn = 2 * math.pi * ((j * q) % 16) / 16
    return round(math.cos(turn), 12), round(math.sin(turn), 12)


def weighted(terms):
    total = None
    for scale, value in terms:
        if scale == 0.0:
            continue
        part = value if scale == 1.0 else -value if scale == -1.0 else scale * value
        total = part if total is None else total + part
    return total


def filter_kernel(
    place_ref, *refs,
):
    (
        skip_ref, sources, out_ref,
        (drive, gate, left, right, h_ref, high_ref, low_ref, twist_ref, piece_ref, sems),
    ) = refs[0], refs[1:9], refs[9], refs[10:]
    targets = [piece_ref.at[k] for k in range(4)] + [h_ref, high_ref, low_ref, twist_ref]
    copies = copy_all(zip(sources, targets), sems)
    tables = copies[4:]
    for copy in copies[:4]:
        copy.wait()

    def transform():
        for part in range(2):
            values = left[part]
            high = values.astype(jnp.bfloat16)
            low = (values - high.astype(jnp.float32)).astype(jnp.bfloat16)
            right[part] = sum(
                jnp.dot(a, b[...], preferred_element_type=jnp.float32)
                for a, b in ((high, high_ref), (high, low_ref), (low, high_ref))
            )

    z, own = place_ref[0], place_ref[2]
    for side, core in enumerate((own, 1 - own)):
        spots = block_spots(core, z)
        for q, (index, column) in zip(spots, ((0, 0), (0, 256), (1, 0), (1, 256))):
            total = piece_ref[2 * side + index, :, column : column + 256]
            gate[q] = total[0:32]
            drive[q] = total[32:64] * total[64:96]
    signal = [drive[q] for q in range(8)]
    for table in tables:
        table.wait()
    for j in range(HALF_CLASSES):
        rows = slice(32 * j, 32 * j + 32)
        cos, sin = twist_ref[j, :, 0:256], twist_ref[j, :, 256:512]
        real = weighted([(small(j, q)[0], signal[q]) for q in range(8)])
        imag = weighted([(-small(j, q)[1], signal[q]) for q in range(8)])
        if imag is None:
            left[0, rows] = real * cos
            left[1, rows] = -real * sin
        else:
            left[0, rows] = real * cos + imag * sin
            left[1, rows] = imag * cos - real * sin
    transform()
    for j in range(HALF_CLASSES):
        rows = slice(32 * j, 32 * j + 32)
        h_real = h_ref[j // 2, 0, j % 2].astype(jnp.float32)
        h_imag = h_ref[j // 2, 1, j % 2].astype(jnp.float32)
        if 0 < j < 8:
            h_real = h_real + h_ref[(16 - j) // 2, 0, j % 2].astype(jnp.float32)
            h_imag = h_imag - h_ref[(16 - j) // 2, 1, j % 2].astype(jnp.float32)
        real = right[0, rows, 0:256] + right[1, rows, 256:512]
        imag = right[1, rows, 0:256] - right[0, rows, 256:512]
        left[0, rows] = real * h_real - imag * h_imag
        left[1, rows] = real * h_imag + imag * h_real
    transform()
    reals, imags = [], []
    for j in range(HALF_CLASSES):
        rows = slice(32 * j, 32 * j + 32)
        cos, sin = twist_ref[j, :, 0:256], twist_ref[j, :, 256:512]
        real = right[0, rows, 0:256] - right[1, rows, 256:512]
        imag = right[1, rows, 0:256] + right[0, rows, 256:512]
        reals.append(real * cos - imag * sin)
        imags.append(real * sin + imag * cos)
    skip = skip_ref[...]
    for q in range(8):
        terms = [(small(j, q)[0], reals[j]) for j in range(HALF_CLASSES)]
        terms += [(-small(j, q)[1], imags[j]) for j in range(HALF_CLASSES)]
        convolved = weighted(terms) * (1.0 / 4096)
        out_ref[q] = (gate[q] * (convolved + skip * drive[q])).astype(out_ref.dtype)


def filtered(where, pieces, spectrum, skip):
    high, low, twist = tables()
    vmem = pl.BlockSpec(memory_space=pltpu.VMEM)
    return pl.pallas_call(
        filter_kernel,
        out_shape=jax.ShapeDtypeStruct((8, 32, 256), jnp.bfloat16),
        in_specs=[pl.BlockSpec(memory_space=pltpu.SMEM)]
        + [vmem]
        + [pl.BlockSpec(memory_space=pl.ANY)] * 8,
        out_specs=vmem,
        scratch_shapes=[
            pltpu.VMEM((8, 32, 256), jnp.float32),
            pltpu.VMEM((8, 32, 256), jnp.float32),
            pltpu.VMEM((2, 32 * HALF_CLASSES, 256), jnp.float32),
            pltpu.VMEM((2, 32 * HALF_CLASSES, 512), jnp.float32),
            pltpu.VMEM((8, 2, 2, 32, 256), jnp.bfloat16),
            pltpu.VMEM((256, 512), jnp.bfloat16),
            pltpu.VMEM((256, 512), jnp.bfloat16),
            pltpu.VMEM((HALF_CLASSES, 1, 512), jnp.float32),
            pltpu.VMEM((4, 96, 512), jnp.float32),
            pltpu.SemaphoreType.DMA((8,)),
        ],
        compiler_params=pltpu.CompilerParams(vmem_limit_bytes=16 * 1024 * 1024),
        cost_estimate=cost(3),
    )(where, skip, *pieces, spectrum, high, low, twist)


def turned_filter(filter_spectrum):
    first = 2 * (NC * lax.axis_index("x") + lax.axis_index("core"))
    eye = np.eye(256, dtype=np.float32)
    own = first + jnp.arange(2, dtype=jnp.int32)
    order = jnp.where((own <= 8)[:, None, None], eye[None], eye[None, :, ::-1])
    turned = jnp.einsum(
        "plgc,lgh->plch",
        filter_spectrum.astype(jnp.bfloat16),
        order.astype(jnp.bfloat16),
        preferred_element_type=jnp.float32,
    ).astype(jnp.bfloat16)
    return turned.reshape(2, 2, 8, 32, 256).transpose(2, 0, 1, 3, 4)


def block_spots(core, z):
    side = jnp.where(z % 2 == 0, 3, 1)
    quarters = [z // 2, z // 2 + side, z // 2 + 4 - side, z // 2 + 2]
    return [2 * (quarter % 4) + core for quarter in quarters]


def cost(microseconds):
    return pl.CostEstimate(
        flops=int(microseconds * 1e9), bytes_accessed=int(microseconds * 3e6), transcendentals=0
    )


def turn_kernel(place_ref, own_ref, sibling_ref, hbm_ref, turned, out_ref, sems):
    z, y, core, x = (place_ref[i] for i in range(4))

    def turn(piece, carry):
        half, k = piece // 4, piece % 4
        own = (z + half) % 2 == core

        def put(ref):
            for part in range(3):
                turned[part] = ref[part, (y + k) % 4].T

        pl.when(own)(lambda: put(own_ref))
        pl.when(jnp.logical_not(own))(lambda: put(sibling_ref))
        columns = pl.ds(pl.multiple_of(256 * k, 256), 256)
        for k_out in range(4):
            for side in range(2):
                start = pl.multiple_of(32 * (2 * ((x + k_out) % 4) + (core + side) % 2), 32)
                for part in range(3):
                    row = 192 * k_out + 96 * side + 32 * part
                    out_ref[half, row : row + 32, columns] = turned[part, pl.ds(start, 32)]
        return carry

    lax.fori_loop(0, 8, turn, 0)
    copies = copy_all([(out_ref.at[half], hbm_ref.at[half]) for half in range(2)], sems)
    for copy in copies:
        copy.wait()


def turned_weight(where, own, sibling):
    vmem = pl.BlockSpec(memory_space=pltpu.VMEM)
    return pl.pallas_call(
        turn_kernel,
        out_shape=jax.ShapeDtypeStruct((2, 768, 1024), jnp.bfloat16),
        in_specs=[pl.BlockSpec(memory_space=pltpu.SMEM), vmem, vmem],
        out_specs=pl.BlockSpec(memory_space=pltpu.HBM),
        scratch_shapes=[
            pltpu.VMEM((3, 256, 256), jnp.bfloat16),
            pltpu.VMEM((2, 768, 1024), jnp.bfloat16),
            pltpu.SemaphoreType.DMA((2,)),
        ],
        compiler_params=pltpu.CompilerParams(vmem_limit_bytes=16 * 1024 * 1024),
        cost_estimate=cost(3),
    )(where, own.reshape(3, 4, 256, 256), sibling.reshape(3, 4, 256, 256))


def copy_all(pairs, sems):
    copies = [
        pltpu.make_async_copy(source, target, sems.at[index])
        for index, (source, target) in enumerate(pairs)
    ]
    for copy in copies:
        copy.start()
    return copies


def join_kernel(*refs):
    parts, out_refs = refs[:4], refs[4:6]
    for k, part in enumerate(parts):
        for half, out_ref in enumerate(out_refs):
            out_ref[:, 256 * k : 256 * k + 256] = part[128 * half : 128 * half + 128]


def joined(parts):
    vmem = pl.BlockSpec(memory_space=pltpu.VMEM)
    return pl.pallas_call(
        join_kernel,
        out_shape=[jax.ShapeDtypeStruct((128, 1024), jnp.bfloat16)] * 2,
        in_specs=[vmem] * 4,
        out_specs=[vmem] * 2,
        cost_estimate=cost(2),
    )(*parts)


def slot_kernel(blocks, count, place_ref, *refs):
    sources, out_refs = refs[: 2 * count + 1], refs[2 * count + 1 : 2 * count + 5]
    unit_ref, weight_ref, sems = refs[2 * count + 5 :]
    pairs = [
        (sources[index], unit_ref.at[index // 2, pl.ds(128 * (index % 2), 128)])
        for index in range(2 * count)
    ]
    copies = copy_all(pairs + [(sources[-1], weight_ref)], sems)
    for copy in copies:
        copy.wait()

    odd = place_ref[0] % 2

    def run(index, carry):
        total = 0.0
        for half in range(2):
            unit = 0
            for number, block in enumerate(blocks):
                even_unit, odd_unit = (
                    [name for name, side in case if side == half][0] for case in block
                )
                unit = jnp.where(index == number, jnp.where(odd, odd_unit, even_unit), unit)
            total += lax.dot_general(
                weight_ref[half], unit_ref[unit], (((1,), (1,)), ((), ())),
                preferred_element_type=jnp.float32,
            )
        columns = pl.ds(pl.multiple_of(256 * index, 256), 256)
        for k, out_ref in enumerate(out_refs):
            rows = slice(192 * k, 192 * k + 192)
            out_ref[:, columns] = total[rows].astype(out_ref.dtype)
        return carry

    lax.fori_loop(0, len(blocks), run, 0)


def slot(where, units, weight, *blocks):
    names = sorted({name for block in blocks for case in block for name, _ in case})
    order = {name: index for index, name in enumerate(names)}
    blocks = [[[(order[name], half) for name, half in case] for case in block] for block in blocks]
    vmem = pl.BlockSpec(memory_space=pltpu.VMEM)
    anywhere = pl.BlockSpec(memory_space=pl.ANY)
    shape = (192, 256 * len(blocks))
    return pl.pallas_call(
        functools.partial(slot_kernel, blocks, len(names)),
        out_shape=[jax.ShapeDtypeStruct(shape, jnp.float32)]
        + [jax.ShapeDtypeStruct(shape, jnp.bfloat16)] * 3,
        in_specs=[pl.BlockSpec(memory_space=pltpu.SMEM)]
        + [anywhere] * (2 * len(names))
        + [pl.BlockSpec(memory_space=pltpu.HBM)],
        out_specs=[vmem] * 4,
        scratch_shapes=[
            pltpu.VMEM((len(names), 256, 1024), jnp.bfloat16),
            pltpu.VMEM((2, 768, 1024), jnp.bfloat16),
            pltpu.SemaphoreType.DMA((2 * len(names) + 1,)),
        ],
        compiler_params=pltpu.CompilerParams(vmem_limit_bytes=16 * 1024 * 1024),
        cost_estimate=cost(3),
    )(where, *[half for name in names for half in units[name]], weight)


def moved_over_x(parts):
    return [shift(parts[k], "x", k) for k in (1, 2, 3)]


def sum_over_x(own, moved):
    total = own
    for part in moved:
        total = total + part.astype(jnp.float32)
    return total[:96], shift(total[96:], "core", 1)


def mix_kernel(place_ref, *refs):
    blocks, weights, out_ref, ordered = refs[:8], refs[8:10], refs[10], refs[11]
    z, core = place_ref[0], place_ref[2]
    for k, step in enumerate((0, 1, 2, 7, 6, 3, 5, 4)):
        ordered[(z + step + 4 * core) % 8] = blocks[k][...]

    def mix_column(column, carry):
        total = sum(
            jnp.dot(
                ordered[4 * side + row], weights[side][column, row],
                preferred_element_type=jnp.float32,
            )
            for side in range(2)
            for row in range(4)
        )
        out_ref[column] = total.astype(out_ref.dtype)
        return carry

    lax.fori_loop(0, 4, mix_column, 0)


def mix(where, blocks, weights):
    vmem = pl.BlockSpec(memory_space=pltpu.VMEM)
    return pl.pallas_call(
        mix_kernel,
        out_shape=jax.ShapeDtypeStruct((4, 256, 256), jnp.bfloat16),
        in_specs=[pl.BlockSpec(memory_space=pltpu.SMEM)] + [vmem] * 10,
        out_specs=vmem,
        scratch_shapes=[pltpu.VMEM((8, 256, 256), jnp.bfloat16)],
        compiler_params=pltpu.CompilerParams(vmem_limit_bytes=16 * 1024 * 1024),
        cost_estimate=cost(2),
    )(where, *blocks, *weights)


def over_ctx(values):
    return lax.all_to_all(values, CTX, split_axis=0, concat_axis=0, tiled=True)


def shards(tokens, in_weight, filter_spectrum, skip_gain, out_weight):
    x, core = lax.axis_index("x"), lax.axis_index("core")
    z, y = lax.axis_index("z"), lax.axis_index("y")
    where = jnp.stack([z, y, core, x]).astype(jnp.int32)

    block = lax.ppermute(tokens, EVERY, MOVE)
    sibling = shift(in_weight, "core", 1)
    sent_filter = turned_filter(filter_spectrum)
    skip = lax.dynamic_slice_in_dim(skip_gain, 32 * (NC * x + core), 32)[:, None]
    spectrum = over_ctx(sent_filter)
    blocks = [block] + [shift(block, "y", -k) for k in (1, 2, 3)]

    out_weight, _ = together(out_weight, block)
    mine = lax.dynamic_index_in_dim(
        out_weight.reshape(2, 4, 4, 256, 256), core, 0, keepdims=False
    )
    rows = [
        lax.dynamic_index_in_dim(mine, (y + 4 - k) % 4, 1, keepdims=False) for k in range(4)
    ]
    halves = joined(blocks)
    spectrum, halves, rows = together(spectrum, halves, rows)
    units = {"own": halves}
    up, down = ([shift(half, "z", step) for half in halves] for step in (1, -1))
    units["up1"], units["down1"] = up, down
    rows[1] = shift(rows[1], "y", -1)

    weight = turned_weight(where, in_weight, sibling)
    weight, last = together(weight, [up[1], down[1]])
    up, down = (
        [shift(first, "z", step), shift(second, "z", step)]
        for first, second, step in ((up[0], last[0], 1), (down[0], last[1], -1))
    )
    units["up2"], units["down2"] = up, down

    rows[1], rows[3], last = together(rows[1], rows[3], [up[1], down[1]])
    rows[3] = shift(rows[3], "y", -3)
    up, down = (
        [shift(first, "z", step), shift(second, "z", step)]
        for first, second, step in ((up[0], last[0], 1), (down[0], last[1], -1))
    )
    units["up3"], units["down3"] = up, down
    parts = slot(
        where, units, weight,
        [[("own", 0), ("down1", 1)], [("own", 0), ("up1", 1)]],
        [[("up1", 1), ("up2", 0)], [("down1", 1), ("down2", 0)]],
    )
    parts, rows[3], last = together(parts, rows[3], down[1])
    early, _ = together(parts, [up[1], down[0]])
    moved = moved_over_x(early)

    units["across"] = [shift(up[0], "z", 1), shift(last, "z", -1)]
    parts = slot(
        where, units, weight,
        [[("down2", 0), ("down3", 1)], [("up2", 0), ("up3", 1)]],
        [[("up3", 1), ("across", 0)], [("down3", 1), ("across", 0)]],
    )
    rows[2], _ = together(rows[2], parts[0])
    rows[2] = shift(rows[2], "y", -2)
    parts, moved = together(parts, moved)
    pieces = [sum_over_x(early[0], moved), sum_over_x(parts[0], moved_over_x(parts))]
    pieces = [piece[0] for piece in pieces] + [piece[1] for piece in pieces]

    gated = filtered(where, pieces, spectrum, skip)
    gated, rows[2] = together(gated, rows[2])
    gated = over_ctx(gated).reshape(256, 256).T
    rows, _ = together(rows, gated)
    rows = jnp.stack(rows)
    partial = mix(where, near_and_far(gated), [rows, shift(rows, "core", 1)])
    total = partial[0].astype(jnp.float32)
    for k in (1, 2, 3):
        total = total + shift(partial[k], "y", k).astype(jnp.float32)
    return total.astype(jnp.bfloat16)


def solution(mesh):
    fine = Mesh(mesh.devices.reshape(NX, NC, NZ, NY), EVERY)
    tp = ("z", "y")
    placed = (P(CTX, tp), P(None, CTX, tp), P(None, CTX, None, tp), P(tp), P(None, tp))
    return jax.shard_map(
        shards, mesh=fine, in_specs=placed, out_specs=P(CTX, tp), check_vma=False
    )
```
